128 devices in a mesh: wide: 64 (over x, z, y), narrow: 2 (over core).
Axes of the slice: x: 4, y: 4, z: 4, core: 2. Of those that a mesh axis runs over, the one named last changes fastest.
Arguments:
- node_feats: bfloat16 [65536, 256], P('wide'), may hold values from -6 to 6
- send_block: int32 [64, 64, 2, 2], P('wide', None, 'narrow'), may hold values from 0 to 7
- recv_block: int32 [64, 2, 64, 2], P('wide', 'narrow'), may hold values from 0 to 15
- tile_count: int32 [64, 2, 64], P('wide', 'narrow'), may hold values from 0 to 2, as said below
- mask_bits: int32 [64, 2, 64, 2, 9, 128], P('wide', 'narrow'), may hold values from 0 to 32767, as said below
- degree: int32 [262144], P(('wide', 'narrow')), may hold values from 64 to 512
- weight_in: bfloat16 [256, 512], replicated, may hold values from -0.375 to 0.375
- weight_out: bfloat16 [512, 256], replicated, may hold values from -0.25 to 0.25
- norm_gain: float32 [256], replicated, may hold values from 0.1 to 1.9
- cotangent: bfloat16 [65536, 256], P('wide'), may hold values from -6 to 6
Outputs:
- updated: bfloat16 [65536, 256], P('wide')
- grad_nodes: float32 [65536, 256], P('wide')
- grad_weight_in: float32 [256, 512], replicated
- grad_weight_out: float32 [512, 256], replicated
- grad_gain: float32 [256], replicated
The draws below stay inside these ranges and needn't reach their ends.
Inputs may be any that keep to these rules, and one draw needn't show every extreme that they name: `tile_count`: at most 2; in every draw some hyperedge device holds 2 tiles from every node owner. `mask_bits`: no bit stands for a row at or past 128.
All inputs are finite; a program needn't handle non-finite values.
Results may differ from the reference program's by a relative error of at most 0.008.
Values may be sent and summed in bfloat16 or wider, within the bound.
No kernel may reach another device: no remote copies, remote signals or barrier semaphores. Data moves between devices by JAX's collectives and lax.ppermute only.
A program may use at most 192 MiB of HBM per device.

```python
import jax
import jax.numpy as jnp
from jax import lax

WIDTH = 256
MLP_WIDTH = 512
TILE_ROWS = 128
MASK_WORDS = 9
CAPACITY = 2
NODE_BLOCKS = 8
EDGE_BLOCKS = 16
NODES = 65536
HYPEREDGES = 262144
N_WIDE = 64
N_NARROW = 2


def draw_tile_count(key, part):
    key = jax.random.fold_in(key, 11)
    key_one, key_two, key_three, key_four = jax.random.split(key, 4)
    levels = jax.random.randint(key_one, (N_WIDE, N_NARROW, 1, 1), 1, 9)
    full_wide = jax.random.randint(key_two, (), 0, N_WIDE)
    full_narrow = jax.random.randint(key_three, (), 0, N_NARROW)
    wide_pos = jnp.arange(N_WIDE).astype(jnp.int32)[:, None, None, None]
    narrow_pos = jnp.arange(N_NARROW).astype(jnp.int32)[None, :, None, None]
    chosen = jnp.logical_and(wide_pos == full_wide, narrow_pos == full_narrow)
    levels = jnp.where(chosen, 8, levels)
    rolls = jax.random.randint(key_four, (N_WIDE, N_NARROW, N_WIDE, CAPACITY), 0, 8)
    return jnp.sum((rolls < levels).astype(jnp.int32), axis=-1)


def draw_mask_bits(key, part):
    key = jax.random.fold_in(key, 7)
    key_one, key_two = jax.random.split(key, 2)
    word_shape = (N_WIDE, N_NARROW, N_WIDE, CAPACITY, MASK_WORDS, TILE_ROWS)
    first_bits = jax.random.randint(key_one, word_shape, 0, 2 ** 15)
    second_bits = jax.random.randint(key_two, word_shape, 0, 2 ** 15)
    merged = jnp.bitwise_and(first_bits, second_bits)
    widths = jnp.minimum(15, TILE_ROWS - 15 * jnp.arange(MASK_WORDS).astype(jnp.int32))
    bit_limit = jnp.left_shift(jnp.ones((MASK_WORDS,), jnp.int32), widths) - 1
    return jnp.bitwise_and(merged, bit_limit[:, None])


def place_ends(entries, key, low, high):
    index_at = [jax.random.randint(jax.random.fold_in(key, axis), (), 0, length) for axis, length in enumerate(entries.shape)]
    widest = entries.shape.index(max(entries.shape))
    neighbour = index_at[:widest] + [(index_at[widest] + 1) % entries.shape[widest]] + index_at[widest + 1:]
    return entries.at[tuple(index_at)].set(low).at[tuple(neighbour)].set(high)


def shard_levels(key, dims, pieces, least, largest):
    level = 1.0
    for position, shards_of in pieces:
        steps = jax.random.uniform(jax.random.fold_in(jax.random.fold_in(key, 6), position), (shards_of,), jnp.float32, least / len(pieces), largest / len(pieces))
        level = level * jnp.repeat(jnp.exp(steps), dims[position] // shards_of).reshape((-1,) + (1,) * (len(dims) - 1 - position))
    return level


def centred(rng, extent, deviation, limit, shards=(), kind=jnp.bfloat16):
    values = deviation * jax.random.normal(rng, extent, jnp.float32)
    if shards:
        values = values * shard_levels(rng, extent, shards, -0.22, 0.18)
    return jnp.clip(values, -limit, limit).astype(kind)


def setup_inputs(seed: int = 0) -> dict:
    arg_keys = jax.random.split(jax.random.key(seed), 11)
    node_feats = centred(arg_keys[0], (NODES, WIDTH), 1.0, 6.0, ((0, 64),))
    send_block = place_ends(jax.random.randint(arg_keys[1], (N_WIDE, N_WIDE, N_NARROW, CAPACITY), 0, NODE_BLOCKS), jax.random.fold_in(arg_keys[1], 1), 0, NODE_BLOCKS - 1).astype(jnp.int32)
    recv_block = place_ends(jax.random.randint(arg_keys[2], (N_WIDE, N_NARROW, N_WIDE, CAPACITY), 0, EDGE_BLOCKS), jax.random.fold_in(arg_keys[2], 1), 0, EDGE_BLOCKS - 1).astype(jnp.int32)
    tile_count = draw_tile_count(jax.random.fold_in(arg_keys[10], 71), 0)
    mask_bits = draw_mask_bits(jax.random.fold_in(arg_keys[10], 71), 0)
    degree = place_ends(jax.random.randint(arg_keys[5], (HYPEREDGES,), 64, 513), jax.random.fold_in(arg_keys[5], 1), 64, 512).astype(jnp.int32)
    weight_in = centred(arg_keys[6], (WIDTH, MLP_WIDTH), WIDTH ** -0.5, 0.375)
    weight_out = centred(arg_keys[7], (MLP_WIDTH, WIDTH), MLP_WIDTH ** -0.5, 0.25)
    norm_gain = jnp.clip(1.0 + 0.18 * jax.random.normal(arg_keys[8], (WIDTH,), jnp.float32), 0.1, 1.9)
    cotangent = centred(arg_keys[9], (NODES, WIDTH), 1.0, 6.0, ((0, 64),))
    return dict(node_feats=node_feats, send_block=send_block, recv_block=recv_block, tile_count=tile_count, mask_bits=mask_bits, degree=degree, weight_in=weight_in, weight_out=weight_out, norm_gain=norm_gain, cotangent=cotangent)


def unpack_bits(mask_words):
    tile_rows = mask_words.shape[-1]
    row_index = jnp.arange(tile_rows).astype(jnp.int32)
    picked = jnp.take(mask_words, row_index // 15, axis=-2)
    shifted = jnp.right_shift(picked, (row_index % 15)[:, None])
    return jnp.bitwise_and(shifted, 1).astype(jnp.bfloat16)

def reference(node_feats, send_block, recv_block, tile_count, mask_bits, degree, weight_in, weight_out, norm_gain, cotangent):
    devices_all = N_WIDE * N_NARROW
    slot_index = jnp.arange(CAPACITY).astype(jnp.int32)
    src_index = jnp.arange(N_WIDE).astype(jnp.int32)
    edge_ids = jnp.arange(EDGE_BLOCKS).astype(jnp.int32)
    node_ids = jnp.arange(NODE_BLOCKS).astype(jnp.int32)
    device_ids = jnp.arange(devices_all).astype(jnp.int32)

    def device_masks(device):
        wide_at = device // N_NARROW
        narrow_at = device % N_NARROW
        live_slots = slot_index[None, :] < tile_count[wide_at, narrow_at][:, None]
        tile_masks = unpack_bits(mask_bits[wide_at, narrow_at]) * live_slots[:, :, None, None].astype(jnp.bfloat16)
        return (wide_at, narrow_at, tile_masks.astype(jnp.float32))

    def to_edges(node_rows):
        blocks = node_rows.reshape(N_WIDE, NODE_BLOCKS, TILE_ROWS, WIDTH)

        def one_device(device):
            wide_at, narrow_at, tile_masks = device_masks(device)
            picked = blocks[src_index[:, None], send_block[:, wide_at, narrow_at, :]].astype(jnp.float32)
            products = jnp.einsum('skrc,skrf->skcf', tile_masks, picked)
            edge_hot = (recv_block[wide_at, narrow_at][:, :, None] == edge_ids).astype(jnp.float32)
            return jnp.einsum('skb,skcf->bcf', edge_hot, products)
        return lax.map(one_device, device_ids).reshape(HYPEREDGES, WIDTH)

    def to_nodes(edge_rows):
        blocks = edge_rows.reshape(devices_all, EDGE_BLOCKS, TILE_ROWS, WIDTH)

        def one_device(total, device):
            wide_at, narrow_at, tile_masks = device_masks(device)
            picked = blocks[device][recv_block[wide_at, narrow_at]].astype(jnp.float32)
            products = jnp.einsum('skrc,skcf->skrf', tile_masks, picked)
            node_hot = (send_block[:, wide_at, narrow_at, :][:, :, None] == node_ids).astype(jnp.float32)
            return (total + jnp.einsum('skb,skrf->sbrf', node_hot, products), None)
        start = jnp.zeros((N_WIDE, NODE_BLOCKS, TILE_ROWS, WIDTH), jnp.float32)
        total, _ = lax.scan(one_device, start, device_ids)
        return total.reshape(NODES, WIDTH)
    edge_scale = lax.rsqrt(degree.astype(jnp.float32))[:, None]
    edge_feats = (to_edges(node_feats) * edge_scale).astype(jnp.bfloat16)
    pre_act = jnp.dot(edge_feats, weight_in, preferred_element_type=jnp.float32)
    activated = jax.nn.silu(pre_act).astype(jnp.bfloat16)
    edge_out = jnp.dot(activated, weight_out, preferred_element_type=jnp.float32).astype(jnp.bfloat16)
    summed = to_nodes(edge_out)
    inv_rms = lax.rsqrt(lax.optimization_barrier(jnp.mean(summed * summed, axis=-1, keepdims=True)) + 1e-05)
    normed = summed * inv_rms
    updated = (node_feats.astype(jnp.float32) + normed * norm_gain).astype(jnp.bfloat16)
    upstream = cotangent.astype(jnp.float32)
    d_normed = upstream * norm_gain
    d_summed = (inv_rms * (d_normed - normed * lax.optimization_barrier(jnp.mean(d_normed * normed, axis=-1, keepdims=True)))).astype(jnp.bfloat16)
    grad_gain = lax.optimization_barrier(jnp.sum(upstream * normed, axis=0)) * NODES ** (-0.5)
    d_edge = to_edges(d_summed).astype(jnp.bfloat16)
    grad_weight_out = jnp.dot(activated.T, d_edge, preferred_element_type=jnp.float32) * HYPEREDGES ** (-0.5)
    d_act = jnp.dot(d_edge, weight_out.T, preferred_element_type=jnp.float32)
    gate_sig = jax.nn.sigmoid(pre_act)
    d_pre = (d_act * gate_sig * (1.0 + pre_act * (1.0 - gate_sig))).astype(jnp.bfloat16)
    grad_weight_in = jnp.dot(edge_feats.T, d_pre, preferred_element_type=jnp.float32) * HYPEREDGES ** (-0.5)
    d_feats = (jnp.dot(d_pre, weight_in.T, preferred_element_type=jnp.float32) * edge_scale).astype(jnp.bfloat16)
    grad_nodes = upstream + to_nodes(d_feats)
    return (updated, grad_nodes, grad_weight_in, grad_weight_out, grad_gain)
```

```python
import functools

import jax
import jax.numpy as jnp
from jax import lax
from jax.experimental import pallas as pl
from jax.experimental.pallas import tpu as pltpu
from jax.sharding import PartitionSpec as P

F32 = jnp.float32
BF16 = jnp.bfloat16
TILE = 128
STEP_OWNERS = 4
PARAMS = pltpu.CompilerParams(vmem_limit_bytes=52 * 1024 * 1024)


def dot(a, b, dims=((1,), (0,))):
    return lax.dot_general(a, b, (dims, ((), ())), preferred_element_type=F32)


def rows_at(block):
    return pl.ds(pl.multiple_of(block * TILE, TILE), TILE)


def unpack_kernel(count_ref, words_ref, bit_ref, mask_ref, mask_t_ref):
    step = pl.program_id(0)
    tiles = words_ref.shape[0]
    row = lax.broadcasted_iota(jnp.int32, (8, TILE), 0)
    for tile in range(tiles):
        slot = tile % 2
        live = count_ref[step * (tiles // 2) + tile // 2] > slot
        words = jnp.where(live, words_ref[tile], 0)
        groups = []
        for first in range(0, TILE, 8):
            low, high = first // 15, (first + 7) // 15
            picked = jnp.broadcast_to(words[low : low + 1], (8, TILE))
            if high != low:
                later = jnp.broadcast_to(words[high : high + 1], (8, TILE))
                picked = jnp.where(row + first >= high * 15, later, picked)
            hit = jnp.bitwise_and(picked, bit_ref[first : first + 8]) != 0
            groups.append(jnp.where(hit, 1.0, 0.0).astype(F32))
        mask = jnp.concatenate(groups, axis=0)
        mask_ref[tile] = mask.astype(BF16)
        mask_t_ref[tile] = mask.T.astype(BF16)


def unpack(count, words):
    tiles = words.shape[0]
    per = 8
    bit = jnp.left_shift(1, lax.broadcasted_iota(jnp.int32, (TILE, TILE), 0) % 15)
    out = jax.ShapeDtypeStruct((tiles, TILE, TILE), BF16)
    block = pl.BlockSpec((per, TILE, TILE), lambda i, c: (i, 0, 0))
    return pl.pallas_call(
        unpack_kernel,
        out_shape=(out, out),
        grid_spec=pltpu.PrefetchScalarGridSpec(
            num_scalar_prefetch=1,
            grid=(tiles // per,),
            in_specs=[
                pl.BlockSpec((per,) + words.shape[1:], lambda i, c: (i, 0, 0)),
                pl.BlockSpec((TILE, TILE), lambda i, c: (0, 0)),
            ],
            out_specs=(block, block),
        ),
        compiler_params=PARAMS,
        cost_estimate=pl.CostEstimate(flops=tiles * 2**18, bytes_accessed=tiles * 2**17, transcendentals=0),
        name="unpack_masks",
    )(count, words, bit)


def select_kernel(send_ref, rows_ref, out_ref):
    step = pl.program_id(0)
    for owner in range(STEP_OWNERS):
        for slot in range(2):
            block = send_ref[(step * STEP_OWNERS + owner) * 2 + slot]
            out_ref[owner, slot * TILE : (slot + 1) * TILE] = rows_ref[rows_at(block)]


def select(send, rows, owners):
    features = rows.shape[1]
    return pl.pallas_call(
        select_kernel,
        out_shape=jax.ShapeDtypeStruct((owners, 2 * TILE, features), BF16),
        grid_spec=pltpu.PrefetchScalarGridSpec(
            num_scalar_prefetch=1,
            grid=(owners // STEP_OWNERS,),
            in_specs=[pl.BlockSpec(rows.shape, lambda i, c: (0, 0))],
            out_specs=pl.BlockSpec((STEP_OWNERS, 2 * TILE, features), lambda i, c: (i, 0, 0)),
        ),
        compiler_params=PARAMS,
        name="select_blocks",
    )(send, rows)


def collect_step(step, recv_ref, arrived_ref, mask_t_ref, acc):
    for owner in range(STEP_OWNERS):
        for slot in range(2):
            tile = owner * 2 + slot
            where = rows_at(recv_ref[step * STEP_OWNERS * 2 + tile])
            acc[where] += dot(mask_t_ref[tile], arrived_ref[owner, slot * TILE : (slot + 1) * TILE])


def spread_step(step, recv_ref, mask_ref, values, out_ref):
    for owner in range(STEP_OWNERS):
        for slot in range(2):
            tile = owner * 2 + slot
            where = rows_at(recv_ref[step * STEP_OWNERS * 2 + tile])
            out_ref[owner, slot * TILE : (slot + 1) * TILE] = dot(mask_ref[tile], values[where]).astype(BF16)


def forward_kernel(
    steps, recv_ref, arrived_ref, mask_t_ref, mask_ref, scale_ref, w_in_ref, w_out_ref,
    out_ref, feats_ref, act_ref, gate_ref, acc, values,
):
    step = pl.program_id(0)

    @pl.when(step == 0)
    def _():
        acc[...] = jnp.zeros_like(acc)

    @pl.when(step < steps)
    def _():
        collect_step(step, recv_ref, arrived_ref, mask_t_ref, acc)

    @pl.when(step == steps - 1)
    def _():
        chunk = 256

        def body(i, carry):
            at = pl.ds(pl.multiple_of(i * chunk, chunk), chunk)
            feats = (acc[at] * scale_ref[at]).astype(BF16)
            feats_ref[at] = feats
            pre = dot(feats, w_in_ref[...])
            sig = jax.nn.sigmoid(pre)
            act = (pre * sig).astype(BF16)
            act_ref[at] = act
            gate_ref[at] = sig * (1.0 + pre * (1.0 - sig))
            values[at] = dot(act, w_out_ref[...]).astype(BF16)
            return carry

        lax.fori_loop(0, acc.shape[0] // chunk, body, 0)

    @pl.when(step >= steps)
    def _():
        spread_step(step - steps, recv_ref, mask_ref, values, out_ref)


def backward_kernel(
    steps, recv_ref, arrived_ref, mask_t_ref, mask_ref, scale_ref, w_in_ref, w_out_ref,
    feats_ref, act_ref, gate_ref, out_ref, acc, values, grads,
):
    step = pl.program_id(0)
    width = feats_ref.shape[1]
    inner = act_ref.shape[1]

    @pl.when(step == 0)
    def _():
        acc[...] = jnp.zeros_like(acc)
        grads[...] = jnp.zeros_like(grads)

    @pl.when(step < steps)
    def _():
        collect_step(step, recv_ref, arrived_ref, mask_t_ref, acc)

    @pl.when(step == steps - 1)
    def _():
        chunk = 256

        def body(i, carry):
            at = pl.ds(pl.multiple_of(i * chunk, chunk), chunk)
            d_edge = acc[at].astype(BF16)
            d_act = dot(d_edge, w_out_ref[...], ((1,), (1,)))
            d_pre = (d_act * gate_ref[at]).astype(BF16)
            values[at] = (dot(d_pre, w_in_ref[...], ((1,), (1,))) * scale_ref[at]).astype(BF16)
            grads[:inner] += dot(act_ref[at], d_edge, ((0,), (0,)))
            in_part = dot(feats_ref[at], d_pre, ((0,), (0,)))
            for piece in range(inner // width):
                first = inner + piece * width
                grads[first : first + width] += in_part[:, piece * width : (piece + 1) * width]
            return carry

        lax.fori_loop(0, acc.shape[0] // chunk, body, 0)

    @pl.when(step >= steps)
    def _():
        spread_step(step - steps, recv_ref, mask_ref, values, out_ref)
        extra = out_ref.shape[1] - 2 * TILE
        for owner in range(STEP_OWNERS):
            first = ((step - steps) * STEP_OWNERS + owner) * extra
            out_ref[owner, 2 * TILE :] = grads[pl.ds(pl.multiple_of(first, extra), extra)].astype(BF16)


def edge_specs(steps, arrived, scale, w_in, w_out):
    per = STEP_OWNERS * 2
    whole = lambda shape: pl.BlockSpec(shape, lambda i, c: (0,) * len(shape))
    return [
        pl.BlockSpec((STEP_OWNERS,) + arrived.shape[1:], lambda i, c: (jnp.minimum(i, steps - 1), 0, 0)),
        pl.BlockSpec((per, TILE, TILE), lambda i, c: (jnp.minimum(i, steps - 1), 0, 0)),
        pl.BlockSpec((per, TILE, TILE), lambda i, c: (jnp.maximum(i - steps, 0), 0, 0)),
        whole(scale.shape),
        whole(w_in.shape),
        whole(w_out.shape),
    ], whole


def edges_forward(recv, arrived, mask_t, mask, scale, w_in, w_out):
    owners = arrived.shape[0]
    steps = owners // STEP_OWNERS
    edges, width, inner = scale.shape[0], w_in.shape[0], w_in.shape[1]
    specs, whole = edge_specs(steps, arrived, scale, w_in, w_out)
    return pl.pallas_call(
        functools.partial(forward_kernel, steps),
        out_shape=(
            jax.ShapeDtypeStruct((owners, 2 * TILE, width), BF16),
            jax.ShapeDtypeStruct((edges, width), BF16),
            jax.ShapeDtypeStruct((edges, inner), BF16),
            jax.ShapeDtypeStruct((edges, inner), F32),
        ),
        grid_spec=pltpu.PrefetchScalarGridSpec(
            num_scalar_prefetch=1,
            grid=(2 * steps,),
            in_specs=specs,
            out_specs=(
                pl.BlockSpec((STEP_OWNERS, 2 * TILE, width), lambda i, c: (jnp.maximum(i - steps, 0), 0, 0)),
                whole((edges, width)),
                whole((edges, inner)),
                whole((edges, inner)),
            ),
            scratch_shapes=[pltpu.VMEM((edges, width), F32), pltpu.VMEM((edges, width), BF16)],
        ),
        compiler_params=PARAMS,
        name="edges_forward",
    )(recv, arrived, mask_t, mask, scale, w_in, w_out)


def edges_backward(recv, arrived, mask_t, mask, scale, w_in, w_out, feats, act, gate):
    owners = arrived.shape[0]
    steps = owners // STEP_OWNERS
    edges, width, inner = scale.shape[0], w_in.shape[0], w_in.shape[1]
    grad_rows = 2 * inner
    extra = grad_rows // owners
    specs, whole = edge_specs(steps, arrived, scale, w_in, w_out)
    return pl.pallas_call(
        functools.partial(backward_kernel, steps),
        out_shape=jax.ShapeDtypeStruct((owners, 2 * TILE + extra, width), BF16),
        grid_spec=pltpu.PrefetchScalarGridSpec(
            num_scalar_prefetch=1,
            grid=(2 * steps,),
            in_specs=specs + [whole(feats.shape), whole(act.shape), whole(gate.shape)],
            out_specs=pl.BlockSpec(
                (STEP_OWNERS, 2 * TILE + extra, width), lambda i, c: (jnp.maximum(i - steps, 0), 0, 0)
            ),
            scratch_shapes=[
                pltpu.VMEM((edges, width), F32),
                pltpu.VMEM((edges, width), BF16),
                pltpu.VMEM((grad_rows, width), F32),
            ],
        ),
        compiler_params=PARAMS,
        name="edges_backward",
    )(recv, arrived, mask_t, mask, scale, w_in, w_out, feats, act, gate)


def gather_sum_kernel(send_ref, arrived_ref, out_ref):
    step = pl.program_id(0)
    nodes = out_ref.shape[0] - (arrived_ref.shape[1] - 2 * TILE)

    @pl.when(step == 0)
    def _():
        out_ref[...] = jnp.zeros_like(out_ref)

    for owner in range(STEP_OWNERS):
        for slot in range(2):
            where = rows_at(send_ref[(step * STEP_OWNERS + owner) * 2 + slot])
            out_ref[where] += arrived_ref[owner, slot * TILE : (slot + 1) * TILE].astype(F32)
        if arrived_ref.shape[1] > 2 * TILE:
            out_ref[nodes:] += arrived_ref[owner, 2 * TILE :].astype(F32)


def gather_sum(send, arrived, nodes):
    owners, rows, width = arrived.shape
    total = nodes + rows - 2 * TILE
    return pl.pallas_call(
        gather_sum_kernel,
        out_shape=jax.ShapeDtypeStruct((total, width), F32),
        grid_spec=pltpu.PrefetchScalarGridSpec(
            num_scalar_prefetch=1,
            grid=(owners // STEP_OWNERS,),
            in_specs=[pl.BlockSpec((STEP_OWNERS, rows, width), lambda i, c: (i, 0, 0))],
            out_specs=pl.BlockSpec((total, width), lambda i, c: (0, 0)),
        ),
        compiler_params=PARAMS,
        name="node_sums",
    )(send, arrived)


def norm_kernel(
    send_ref, mine_ref, other_ref, feats_ref, cot_ref, gain_ref, updated_ref, part_ref, out_ref, d_summed
):
    step = pl.program_id(0)

    @pl.when(step == 0)
    def _():
        gain = gain_ref[...]

        def body(i, part):
            at = rows_at(i)
            summed = mine_ref[at] + other_ref[at]
            inv_rms = lax.rsqrt(jnp.mean(summed * summed, axis=-1, keepdims=True) + 1e-05)
            normed = summed * inv_rms
            updated_ref[at] = (feats_ref[at].astype(F32) + normed * gain).astype(BF16)
            upstream = cot_ref[at].astype(F32)
            d_normed = upstream * gain
            inner = jnp.mean(d_normed * normed, axis=-1, keepdims=True)
            d_summed[at] = (inv_rms * (d_normed - normed * inner)).astype(BF16)
            return part + jnp.sum((upstream * normed).reshape(TILE // 8, 8, -1), axis=0)

        part_ref[...] = lax.fori_loop(0, mine_ref.shape[0] // TILE, body, jnp.zeros_like(part_ref))

    select_kernel(send_ref, d_summed, out_ref)


def norm_and_select(send, mine, other, feats, cot, gain, owners):
    nodes, width = feats.shape
    whole = lambda shape: pl.BlockSpec(shape, lambda i, c: (0,) * len(shape))
    return pl.pallas_call(
        norm_kernel,
        out_shape=(
            jax.ShapeDtypeStruct((nodes, width), BF16),
            jax.ShapeDtypeStruct((8, width), F32),
            jax.ShapeDtypeStruct((owners, 2 * TILE, width), BF16),
        ),
        grid_spec=pltpu.PrefetchScalarGridSpec(
            num_scalar_prefetch=1,
            grid=(owners // STEP_OWNERS,),
            in_specs=[whole((nodes, width))] * 4 + [whole((1, width))],
            out_specs=(
                whole((nodes, width)),
                whole((8, width)),
                pl.BlockSpec((STEP_OWNERS, 2 * TILE, width), lambda i, c: (i, 0, 0)),
            ),
            scratch_shapes=[pltpu.VMEM((nodes, width), BF16)],
        ),
        compiler_params=PARAMS,
        name="norm_and_select",
    )(send, mine, other, feats, cot, gain)


def exchange(rows):
    return lax.all_to_all(rows, "wide", split_axis=0, concat_axis=0, tiled=True)


def swap(rows):
    return lax.ppermute(rows, "narrow", [(0, 1), (1, 0)])


def shards(
    node_feats,
    send_block,
    recv_block,
    tile_count,
    mask_bits,
    degree,
    weight_in,
    weight_out,
    norm_gain,
    cotangent,
):
    owners = lax.axis_size("wide")
    nodes, width = node_feats.shape
    inner = weight_in.shape[1]
    send = send_block.reshape(-1)
    recv = recv_block.reshape(-1)
    count = tile_count.reshape(-1)
    words = mask_bits.reshape((-1,) + mask_bits.shape[4:])
    scale = lax.rsqrt(degree.astype(F32))[:, None]
    gain = norm_gain[None, :]

    mask, mask_t = unpack(count, words)
    arrived = exchange(select(send, node_feats, owners))
    products, feats, act, gate = edges_forward(recv, arrived, mask_t, mask, scale, weight_in, weight_out)
    mine = gather_sum(send, exchange(products), nodes)
    updated, part, picked = norm_and_select(send, mine, swap(mine), node_feats, cotangent, gain, owners)
    products = edges_backward(
        recv, exchange(picked), mask_t, mask, scale, weight_in, weight_out, feats, act, gate
    )
    mine = gather_sum(send, exchange(products), nodes)
    both = mine + swap(mine)
    grad_nodes = cotangent.astype(F32) + both[:nodes]

    core = lax.axis_index("narrow")
    extra = mine.shape[0] - nodes
    half = lax.dynamic_slice_in_dim(both[nodes:], core * (extra // 2), extra // 2, 0)
    chunk = jnp.concatenate([half.reshape(extra, width // 2), part.sum(0).reshape(-1, width // 2)], 0)
    chunk = jnp.pad(chunk, ((0, -chunk.shape[0] % 8), (0, 0)))
    everyone = exchange(jnp.broadcast_to(chunk[None], (owners,) + chunk.shape))
    grad_gain = everyone[:, extra : extra + width // (width // 2)].sum(0).reshape(width)
    halves = everyone[:, :extra].reshape(owners, extra // 2, width)
    theirs = swap(halves)
    lower = jnp.where(core == 0, halves, theirs)
    upper = jnp.where(core == 0, theirs, halves)
    grads = jnp.concatenate([lower, upper], 1).reshape(2 * inner, width)
    pieces = inner // width
    grad_out = grads[:inner]
    grad_in = grads[inner:].reshape(pieces, width, width).transpose(1, 0, 2).reshape(width, inner)

    edge_factor = (degree.shape[0] * owners * lax.axis_size("narrow")) ** (-0.5)
    return (
        updated,
        grad_nodes,
        grad_in * edge_factor,
        grad_out * edge_factor,
        grad_gain * (nodes * owners) ** (-0.5),
    )


def solution(mesh):
    return jax.shard_map(
        shards,
        mesh=mesh,
        in_specs=(
            P("wide", None),
            P("wide", None, "narrow", None),
            P("wide", "narrow", None, None),
            P("wide", "narrow", None),
            P("wide", "narrow", None, None, None, None),
            P(("wide", "narrow")),
            P(),
            P(),
            P(),
            P("wide", None),
        ),
        out_specs=(P("wide", None), P("wide", None), P(), P(), P()),
        check_vma=False,
    )
```

```python
import functools

import jax
import jax.numpy as jnp
from jax import lax
from jax.experimental import pallas as pl
from jax.experimental.pallas import tpu as pltpu
from jax.sharding import PartitionSpec as P

F32 = jnp.float32
BF16 = jnp.bfloat16
TILE = 128
STEP_OWNERS = 4
PARAMS = pltpu.CompilerParams(vmem_limit_bytes=52 * 1024 * 1024)


SMEM = pl.BlockSpec(memory_space=pltpu.SMEM)
VMEM = pl.BlockSpec(memory_space=pltpu.VMEM)
ANY = pl.BlockSpec(memory_space=pl.ANY)


def dot(a, b, dims=((1,), (0,))):
    return lax.dot_general(a, b, (dims, ((), ())), preferred_element_type=F32)


def rows_at(block):
    return pl.ds(pl.multiple_of(block * TILE, TILE), TILE)


def unpack_kernel(count_ref, words_ref, bit_ref, mask_ref, mask_t_ref):
    step = pl.program_id(0)
    tiles = words_ref.shape[0]
    row = lax.broadcasted_iota(jnp.int32, (8, TILE), 0)
    for tile in range(tiles):
        slot = tile % 2
        live = count_ref[step * (tiles // 2) + tile // 2] > slot
        words = jnp.where(live, words_ref[tile], 0)
        groups = []
        for first in range(0, TILE, 8):
            low, high = first // 15, (first + 7) // 15
            picked = jnp.broadcast_to(words[low : low + 1], (8, TILE))
            if high != low:
                later = jnp.broadcast_to(words[high : high + 1], (8, TILE))
                picked = jnp.where(row + first >= high * 15, later, picked)
            hit = jnp.bitwise_and(picked, bit_ref[first : first + 8]) != 0
            groups.append(jnp.where(hit, 1.0, 0.0).astype(F32))
        mask = jnp.concatenate(groups, axis=0)
        mask_ref[tile] = mask.astype(BF16)
        mask_t_ref[tile] = mask.T.astype(BF16)


def unpack(count, words):
    tiles = words.shape[0]
    per = 8
    bit = jnp.left_shift(1, lax.broadcasted_iota(jnp.int32, (TILE, TILE), 0) % 15)
    out = jax.ShapeDtypeStruct((tiles, TILE, TILE), BF16)
    block = pl.BlockSpec((per, TILE, TILE), lambda i, c: (i, 0, 0))
    return pl.pallas_call(
        unpack_kernel,
        out_shape=(out, out),
        grid_spec=pltpu.PrefetchScalarGridSpec(
            num_scalar_prefetch=1,
            grid=(tiles // per,),
            in_specs=[
                pl.BlockSpec((per,) + words.shape[1:], lambda i, c: (i, 0, 0)),
                pl.BlockSpec((TILE, TILE), lambda i, c: (0, 0)),
            ],
            out_specs=(block, block),
        ),
        compiler_params=PARAMS,
        cost_estimate=pl.CostEstimate(flops=tiles * 2**18, bytes_accessed=tiles * 2**17, transcendentals=0),
        name="unpack_masks",
    )(count, words, bit)


def copy(src, dst, sem):
    return pltpu.make_async_copy(src, dst, sem)


def send_blocks(send_ref, rows_ref, out_ref, sem):
    def body(i, carry):
        copy(rows_ref.at[rows_at(send_ref[i])], out_ref.at[i], sem).start()
        return carry

    lax.fori_loop(0, out_ref.shape[0], body, 0, unroll=8)
    copy(out_ref, out_ref, sem).wait()


def select(send, rows, owners):
    tiles, features = 2 * owners, rows.shape[1]
    out = pl.pallas_call(
        send_blocks,
        out_shape=jax.ShapeDtypeStruct((tiles, TILE, features), BF16),
        in_specs=[SMEM, VMEM],
        out_specs=ANY,
        scratch_shapes=[pltpu.SemaphoreType.DMA],
        compiler_params=PARAMS,
        name="select_blocks",
    )(send, rows)
    return out.reshape(owners, 2 * TILE, features)


def part(ref, i, size):
    return ref.at[pl.ds(i * size, size)]


def start_all(src, dst, sems, size):
    def body(i, carry):
        copy(part(src, i, size), part(dst, i, size), sems.at[i]).start()
        return carry

    lax.fori_loop(0, src.shape[0] // size, body, 0)


def collect(recv_ref, arrived, mask_t, arrived_sems, mask_sems, arrived_ref, mask_t_ref, acc):
    per = 2 * STEP_OWNERS

    def body(i, carry):
        copy(part(arrived_ref, i, STEP_OWNERS), part(arrived, i, STEP_OWNERS), arrived_sems.at[i]).wait()
        copy(part(mask_t_ref, i, per), part(mask_t, i, per), mask_sems.at[i]).wait()
        for tile in range(per):
            where = rows_at(recv_ref[i * per + tile])
            rows = arrived[i * STEP_OWNERS + tile // 2, tile % 2 * TILE : (tile % 2 + 1) * TILE]
            acc[where] += dot(mask_t[i * per + tile], rows)
        return carry

    lax.fori_loop(0, arrived.shape[0] // STEP_OWNERS, body, 0)


def spread(recv_ref, mask, mask_sems, mask_ref, values, made, out_ref, sem, grads=None):
    per = 2 * STEP_OWNERS

    def body(i, carry):
        copy(part(mask_ref, i, per), part(mask, i, per), mask_sems.at[i]).wait()
        for tile in range(per):
            where = rows_at(recv_ref[i * per + tile])
            owner = i * STEP_OWNERS + tile // 2
            made[owner, tile % 2 * TILE : (tile % 2 + 1) * TILE] = dot(mask[i * per + tile], values[where]).astype(BF16)
            if grads is not None and tile % 2:
                extra = made.shape[1] - 2 * TILE
                made[owner, 2 * TILE :] = grads[pl.ds(pl.multiple_of(owner * extra, extra), extra)].astype(BF16)
        copy(part(made, i, STEP_OWNERS), part(out_ref, i, STEP_OWNERS), sem).start()
        return carry

    lax.fori_loop(0, made.shape[0] // STEP_OWNERS, body, 0)


def forward_kernel(
    recv_ref, arrived_ref, mask_t_ref, mask_ref, scale_ref, w_in_ref, w_out_ref,
    out_ref, feats_ref, act_ref, gate_ref,
    arrived, mask_t, mask, made, acc, values, feats, act, gate, sems, out_sems,
):
    per = 2 * STEP_OWNERS
    start_all(arrived_ref, arrived, sems.at[0], STEP_OWNERS)
    start_all(mask_t_ref, mask_t, sems.at[1], per)
    start_all(mask_ref, mask, sems.at[2], per)
    acc[...] = jnp.zeros_like(acc)
    collect(recv_ref, arrived, mask_t, sems.at[0], sems.at[1], arrived_ref, mask_t_ref, acc)
    chunk = 256

    def body(i, carry):
        at = pl.ds(pl.multiple_of(i * chunk, chunk), chunk)
        rows = (acc[at] * scale_ref[at]).astype(BF16)
        feats[at] = rows
        pre = dot(rows, w_in_ref[...])
        sig = jax.nn.sigmoid(pre)
        hidden = (pre * sig).astype(BF16)
        act[at] = hidden
        gate[at] = sig * (1.0 + pre * (1.0 - sig))
        values[at] = dot(hidden, w_out_ref[...]).astype(BF16)
        for k, (mine, out) in enumerate(((feats, feats_ref), (act, act_ref), (gate, gate_ref))):
            copy(mine.at[at], out.at[at], out_sems.at[k]).start()
        return carry

    lax.fori_loop(0, acc.shape[0] // chunk, body, 0)
    spread(recv_ref, mask, sems.at[2], mask_ref, values, made, out_ref, out_sems.at[3])
    for k, (mine, out) in enumerate(((feats, feats_ref), (act, act_ref), (gate, gate_ref), (made, out_ref))):
        copy(mine, out, out_sems.at[k]).wait()


def backward_kernel(
    recv_ref, arrived_ref, mask_t_ref, mask_ref, scale_ref, w_in_ref, w_out_ref,
    feats_ref, act_ref, gate_ref, out_ref,
    arrived, mask_t, mask, made, acc, values, feats, act, gate, grads, sems, in_sems,
):
    width, inner = feats.shape[1], act.shape[1]
    per = 2 * STEP_OWNERS
    start_all(arrived_ref, arrived, sems.at[0], STEP_OWNERS)
    start_all(mask_t_ref, mask_t, sems.at[1], per)
    kept = ((feats_ref, feats), (act_ref, act), (gate_ref, gate))
    for k, (src, dst) in enumerate(kept):
        copy(src, dst, in_sems.at[k]).start()
    start_all(mask_ref, mask, sems.at[2], per)
    acc[...] = jnp.zeros_like(acc)
    grads[...] = jnp.zeros_like(grads)
    collect(recv_ref, arrived, mask_t, sems.at[0], sems.at[1], arrived_ref, mask_t_ref, acc)
    for k, (src, dst) in enumerate(kept):
        copy(src, dst, in_sems.at[k]).wait()
    chunk = 256

    def body(i, carry):
        at = pl.ds(pl.multiple_of(i * chunk, chunk), chunk)
        d_edge = acc[at].astype(BF16)
        d_act = dot(d_edge, w_out_ref[...], ((1,), (1,)))
        d_pre = (d_act * gate[at]).astype(BF16)
        values[at] = (dot(d_pre, w_in_ref[...], ((1,), (1,))) * scale_ref[at]).astype(BF16)
        grads[:inner] += dot(act[at], d_edge, ((0,), (0,)))
        in_part = dot(feats[at], d_pre, ((0,), (0,)))
        for piece in range(inner // width):
            first = inner + piece * width
            grads[first : first + width] += in_part[:, piece * width : (piece + 1) * width]
        return carry

    lax.fori_loop(0, acc.shape[0] // chunk, body, 0)
    spread(recv_ref, mask, sems.at[2], mask_ref, values, made, out_ref, in_sems.at[3], grads)
    copy(made, out_ref, in_sems.at[3]).wait()


def edge_scratch(owners, rows, edges, width, inner):
    tiles = 2 * owners
    steps = owners // STEP_OWNERS
    return [
        pltpu.VMEM((owners, 2 * TILE, width), BF16),
        pltpu.VMEM((tiles, TILE, TILE), BF16),
        pltpu.VMEM((tiles, TILE, TILE), BF16),
        pltpu.VMEM((owners, rows, width), BF16),
        pltpu.VMEM((edges, width), F32),
        pltpu.VMEM((edges, width), BF16),
        pltpu.VMEM((edges, width), BF16),
        pltpu.VMEM((edges, inner), BF16),
        pltpu.VMEM((edges, inner), F32),
    ], [pltpu.SemaphoreType.DMA((3, steps)), pltpu.SemaphoreType.DMA((4,))]


def edges_forward(recv, arrived, mask_t, mask, scale, w_in, w_out):
    owners = arrived.shape[0]
    edges, width, inner = scale.shape[0], w_in.shape[0], w_in.shape[1]
    buffers, sems = edge_scratch(owners, 2 * TILE, edges, width, inner)
    return pl.pallas_call(
        forward_kernel,
        out_shape=(
            jax.ShapeDtypeStruct((owners, 2 * TILE, width), BF16),
            jax.ShapeDtypeStruct((edges, width), BF16),
            jax.ShapeDtypeStruct((edges, inner), BF16),
            jax.ShapeDtypeStruct((edges, inner), F32),
        ),
        in_specs=[SMEM, ANY, ANY, ANY, VMEM, VMEM, VMEM],
        out_specs=(ANY,) * 4,
        scratch_shapes=buffers + sems,
        compiler_params=PARAMS,
        name="edges_forward",
    )(recv, arrived, mask_t, mask, scale, w_in, w_out)


def edges_backward(recv, arrived, mask_t, mask, scale, w_in, w_out, feats, act, gate):
    owners = arrived.shape[0]
    edges, width, inner = scale.shape[0], w_in.shape[0], w_in.shape[1]
    grad_rows = 2 * inner
    extra = grad_rows // owners
    buffers, sems = edge_scratch(owners, 2 * TILE + extra, edges, width, inner)
    return pl.pallas_call(
        backward_kernel,
        out_shape=jax.ShapeDtypeStruct((owners, 2 * TILE + extra, width), BF16),
        in_specs=[SMEM, ANY, ANY, ANY, VMEM, VMEM, VMEM, ANY, ANY, ANY],
        out_specs=ANY,
        scratch_shapes=buffers + [pltpu.VMEM((grad_rows, width), F32)] + sems,
        compiler_params=PARAMS,
        name="edges_backward",
    )(recv, arrived, mask_t, mask, scale, w_in, w_out, feats, act, gate)


def gather_sum_kernel(send_ref, arrived_ref, out_ref, arrived, sems):
    per = 2 * STEP_OWNERS
    blocks = arrived_ref.at[:, pl.ds(0, 2 * TILE)]
    start_all(blocks, arrived, sems, STEP_OWNERS)
    out_ref[...] = jnp.zeros_like(out_ref)

    def body(i, carry):
        copy(part(blocks, i, STEP_OWNERS), part(arrived, i, STEP_OWNERS), sems.at[i]).wait()
        for tile in range(per):
            where = rows_at(send_ref[i * per + tile])
            rows = arrived[i * STEP_OWNERS + tile // 2, tile % 2 * TILE : (tile % 2 + 1) * TILE]
            out_ref[where] += rows.astype(F32)
        return carry

    lax.fori_loop(0, arrived.shape[0] // STEP_OWNERS, body, 0)


def gather_sum(send, arrived, nodes):
    owners, _, width = arrived.shape
    return pl.pallas_call(
        gather_sum_kernel,
        out_shape=jax.ShapeDtypeStruct((nodes, width), F32),
        in_specs=[SMEM, ANY],
        out_specs=VMEM,
        scratch_shapes=[
            pltpu.VMEM((owners, 2 * TILE, width), BF16),
            pltpu.SemaphoreType.DMA((owners // STEP_OWNERS,)),
        ],
        compiler_params=PARAMS,
        name="node_sums",
    )(send, arrived)


def tail_sum_kernel(arrived_ref, out_ref, tails, sem):
    move = copy(arrived_ref.at[:, pl.ds(2 * TILE, tails.shape[1])], tails, sem)
    move.start()
    move.wait()
    out_ref[...] = jnp.sum(tails[...].astype(F32), axis=0)


def tail_sum(arrived):
    owners, rows, width = arrived.shape
    extra = rows - 2 * TILE
    return pl.pallas_call(
        tail_sum_kernel,
        out_shape=jax.ShapeDtypeStruct((extra, width), F32),
        in_specs=[ANY],
        out_specs=VMEM,
        scratch_shapes=[pltpu.VMEM((owners, extra, width), BF16), pltpu.SemaphoreType.DMA],
        compiler_params=PARAMS,
        name="weight_sums",
    )(arrived)


def norm_kernel(
    send_ref, mine_ref, other_ref, feats_ref, cot_ref, gain_ref, updated_ref, part_ref, out_ref, d_summed, sem
):
    gain = gain_ref[...]

    def body(i, part):
        at = rows_at(i)
        summed = mine_ref[at] + other_ref[at]
        inv_rms = lax.rsqrt(jnp.mean(summed * summed, axis=-1, keepdims=True) + 1e-05)
        normed = summed * inv_rms
        updated_ref[at] = (feats_ref[at].astype(F32) + normed * gain).astype(BF16)
        upstream = cot_ref[at].astype(F32)
        d_normed = upstream * gain
        inner = jnp.mean(d_normed * normed, axis=-1, keepdims=True)
        d_summed[at] = (inv_rms * (d_normed - normed * inner)).astype(BF16)
        return part + jnp.sum((upstream * normed).reshape(TILE // 8, 8, -1), axis=0)

    part_ref[...] = lax.fori_loop(0, mine_ref.shape[0] // TILE, body, jnp.zeros_like(part_ref))
    send_blocks(send_ref, d_summed, out_ref, sem)


def norm_and_select(send, mine, other, feats, cot, gain, owners):
    nodes, width = feats.shape
    updated, gain_part, out = pl.pallas_call(
        norm_kernel,
        out_shape=(
            jax.ShapeDtypeStruct((nodes, width), BF16),
            jax.ShapeDtypeStruct((8, width), F32),
            jax.ShapeDtypeStruct((2 * owners, TILE, width), BF16),
        ),
        in_specs=[SMEM] + [VMEM] * 5,
        out_specs=(VMEM, VMEM, ANY),
        scratch_shapes=[pltpu.VMEM((nodes, width), BF16), pltpu.SemaphoreType.DMA],
        compiler_params=PARAMS,
        name="norm_and_select",
    )(send, mine, other, feats, cot, gain)
    return updated, gain_part, out.reshape(owners, 2 * TILE, width)


def exchange(rows):
    return lax.all_to_all(rows, "wide", split_axis=0, concat_axis=0, tiled=True)


def swap(rows):
    return lax.ppermute(rows, "narrow", [(0, 1), (1, 0)])


def shards(
    node_feats,
    send_block,
    recv_block,
    tile_count,
    mask_bits,
    degree,
    weight_in,
    weight_out,
    norm_gain,
    cotangent,
):
    owners = lax.axis_size("wide")
    nodes, width = node_feats.shape
    inner = weight_in.shape[1]
    send = send_block.reshape(-1)
    recv = recv_block.reshape(-1)
    count = tile_count.reshape(-1)
    words = mask_bits.reshape((-1,) + mask_bits.shape[4:])
    scale = lax.rsqrt(degree.astype(F32))[:, None]
    gain = norm_gain[None, :]

    mask, mask_t = unpack(count, words)
    arrived = exchange(select(send, node_feats, owners))
    products, feats, act, gate = edges_forward(recv, arrived, mask_t, mask, scale, weight_in, weight_out)
    mine = gather_sum(send, exchange(products), nodes)
    updated, gain_part, picked = norm_and_select(send, mine, swap(mine), node_feats, cotangent, gain, owners)
    products = edges_backward(
        recv, exchange(picked), mask_t, mask, scale, weight_in, weight_out, feats, act, gate
    )
    arrived = exchange(products)
    weight_sums = tail_sum(arrived)
    weight_sums = weight_sums + swap(weight_sums)
    core = lax.axis_index("narrow")
    extra = weight_sums.shape[0]
    half = lax.dynamic_slice_in_dim(weight_sums, core * (extra // 2), extra // 2, 0)
    chunk = jnp.concatenate([half.reshape(extra, width // 2), gain_part.sum(0).reshape(-1, width // 2)], 0)
    chunk = jnp.pad(chunk, ((0, -chunk.shape[0] % 8), (0, 0)))
    everyone = exchange(jnp.broadcast_to(chunk[None], (owners,) + chunk.shape))
    mine = gather_sum(send, arrived, nodes)
    grad_nodes = cotangent.astype(F32) + (mine + swap(mine))

    grad_gain = everyone[:, extra : extra + 2].sum(0).reshape(width)
    halves = everyone[:, :extra].reshape(owners, extra // 2, width)
    theirs = swap(halves)
    lower = jnp.where(core == 0, halves, theirs)
    upper = jnp.where(core == 0, theirs, halves)
    grads = jnp.concatenate([lower, upper], 1).reshape(2 * inner, width)
    pieces = inner // width
    grad_out = grads[:inner]
    grad_in = grads[inner:].reshape(pieces, width, width).transpose(1, 0, 2).reshape(width, inner)

    edge_factor = (degree.shape[0] * owners * lax.axis_size("narrow")) ** (-0.5)
    return (
        updated,
        grad_nodes,
        grad_in * edge_factor,
        grad_out * edge_factor,
        grad_gain * (nodes * owners) ** (-0.5),
    )


def solution(mesh):
    return jax.shard_map(
        shards,
        mesh=mesh,
        in_specs=(
            P("wide", None),
            P("wide", None, "narrow", None),
            P("wide", "narrow", None, None),
            P("wide", "narrow", None),
            P("wide", "narrow", None, None, None, None),
            P(("wide", "narrow")),
            P(),
            P(),
            P(),
            P("wide", None),
        ),
        out_specs=(P("wide", None), P("wide", None), P(), P(), P()),
        check_vma=False,
    )
```

```python
import functools

import jax
import jax.numpy as jnp
from jax import lax
from jax.experimental import pallas as pl
from jax.experimental.pallas import tpu as pltpu
from jax.sharding import PartitionSpec as P

F32 = jnp.float32
BF16 = jnp.bfloat16
TILE = 128
STEP_OWNERS = 4
PARAMS = pltpu.CompilerParams(vmem_limit_bytes=52 * 1024 * 1024)


SMEM = pl.BlockSpec(memory_space=pltpu.SMEM)
VMEM = pl.BlockSpec(memory_space=pltpu.VMEM)
ANY = pl.BlockSpec(memory_space=pl.ANY)


def dot(a, b, dims=((1,), (0,))):
    return lax.dot_general(a, b, (dims, ((), ())), preferred_element_type=F32)


def rows_at(block):
    return pl.ds(pl.multiple_of(block * TILE, TILE), TILE)


def unpack_kernel(count_ref, words_ref, bit_ref, mask_ref, mask_t_ref):
    step = pl.program_id(0)
    tiles = words_ref.shape[0]
    row = lax.broadcasted_iota(jnp.int32, (8, TILE), 0)
    for tile in range(tiles):
        slot = tile % 2
        live = count_ref[step * (tiles // 2) + tile // 2] > slot
        words = jnp.where(live, words_ref[tile], 0)
        groups = []
        for first in range(0, TILE, 8):
            low, high = first // 15, (first + 7) // 15
            picked = jnp.broadcast_to(words[low : low + 1], (8, TILE))
            if high != low:
                later = jnp.broadcast_to(words[high : high + 1], (8, TILE))
                picked = jnp.where(row + first >= high * 15, later, picked)
            hit = jnp.bitwise_and(picked, bit_ref[first : first + 8]) != 0
            groups.append(jnp.where(hit, 1.0, 0.0).astype(F32))
        mask = jnp.concatenate(groups, axis=0)
        mask_ref[tile] = mask.astype(BF16)
        mask_t_ref[tile] = mask.T.astype(BF16)


def unpack(count, words):
    tiles = words.shape[0]
    per = 8
    bit = jnp.left_shift(1, lax.broadcasted_iota(jnp.int32, (TILE, TILE), 0) % 15)
    out = jax.ShapeDtypeStruct((tiles, TILE, TILE), BF16)
    block = pl.BlockSpec((per, TILE, TILE), lambda i, c: (i, 0, 0))
    return pl.pallas_call(
        unpack_kernel,
        out_shape=(out, out),
        grid_spec=pltpu.PrefetchScalarGridSpec(
            num_scalar_prefetch=1,
            grid=(tiles // per,),
            in_specs=[
                pl.BlockSpec((per,) + words.shape[1:], lambda i, c: (i, 0, 0)),
                pl.BlockSpec((TILE, TILE), lambda i, c: (0, 0)),
            ],
            out_specs=(block, block),
        ),
        compiler_params=PARAMS,
        cost_estimate=pl.CostEstimate(flops=tiles * 2**18, bytes_accessed=tiles * 2**17, transcendentals=0),
        name="unpack_masks",
    )(count, words, bit)


def copy(src, dst, sem):
    return pltpu.make_async_copy(src, dst, sem)


def send_blocks(send_ref, rows_ref, out_ref, sem):
    def body(i, carry):
        copy(rows_ref.at[rows_at(send_ref[i])], out_ref.at[i], sem).start()
        return carry

    lax.fori_loop(0, out_ref.shape[0], body, 0, unroll=8)
    copy(out_ref, out_ref, sem).wait()


def select(send, rows, owners):
    tiles, features = 2 * owners, rows.shape[1]
    out = pl.pallas_call(
        send_blocks,
        out_shape=jax.ShapeDtypeStruct((tiles, TILE, features), BF16),
        in_specs=[SMEM, VMEM],
        out_specs=ANY,
        scratch_shapes=[pltpu.SemaphoreType.DMA],
        compiler_params=PARAMS,
        name="select_blocks",
    )(send, rows)
    return out.reshape(owners, 2 * TILE, features)


def part(ref, i, size):
    return ref.at[pl.ds(i * size, size)]


def start_all(src, dst, sems, size):
    def body(i, carry):
        copy(part(src, i, size), part(dst, i, size), sems.at[i]).start()
        return carry

    lax.fori_loop(0, src.shape[0] // size, body, 0)


def collect(recv_ref, arrived, mask_t, arrived_sems, mask_sems, arrived_ref, mask_t_ref, acc):
    per = 2 * STEP_OWNERS

    def body(i, carry):
        copy(part(arrived_ref, i, STEP_OWNERS), part(arrived, i, STEP_OWNERS), arrived_sems.at[i]).wait()
        copy(part(mask_t_ref, i, per), part(mask_t, i, per), mask_sems.at[i]).wait()
        for tile in range(per):
            where = rows_at(recv_ref[i * per + tile])
            rows = arrived[i * STEP_OWNERS + tile // 2, tile % 2 * TILE : (tile % 2 + 1) * TILE]
            acc[where] += dot(mask_t[i * per + tile], rows)
        return carry

    lax.fori_loop(0, arrived.shape[0] // STEP_OWNERS, body, 0)


def spread(recv_ref, mask, mask_sems, mask_ref, values, made, out_ref, sem):
    per = 2 * STEP_OWNERS

    def body(i, carry):
        copy(part(mask_ref, i, per), part(mask, i, per), mask_sems.at[i]).wait()
        for tile in range(per):
            where = rows_at(recv_ref[i * per + tile])
            owner = i * STEP_OWNERS + tile // 2
            made[owner, tile % 2 * TILE : (tile % 2 + 1) * TILE] = dot(mask[i * per + tile], values[where]).astype(BF16)
        copy(part(made, i, STEP_OWNERS), part(out_ref, i, STEP_OWNERS), sem).start()
        return carry

    lax.fori_loop(0, made.shape[0] // STEP_OWNERS, body, 0)


def forward_kernel(
    recv_ref, arrived_ref, mask_t_ref, mask_ref, scale_ref, w_in_ref, w_out_ref,
    out_ref, feats_ref, act_ref, gate_ref,
    arrived, mask_t, mask, made, acc, values, feats, act, gate, sems, out_sems,
):
    per = 2 * STEP_OWNERS
    start_all(arrived_ref, arrived, sems.at[0], STEP_OWNERS)
    start_all(mask_t_ref, mask_t, sems.at[1], per)
    start_all(mask_ref, mask, sems.at[2], per)
    acc[...] = jnp.zeros_like(acc)
    collect(recv_ref, arrived, mask_t, sems.at[0], sems.at[1], arrived_ref, mask_t_ref, acc)
    chunk = 256

    def body(i, carry):
        at = pl.ds(pl.multiple_of(i * chunk, chunk), chunk)
        rows = (acc[at] * scale_ref[at]).astype(BF16)
        feats[at] = rows
        pre = dot(rows, w_in_ref[...])
        sig = jax.nn.sigmoid(pre)
        hidden = (pre * sig).astype(BF16)
        act[at] = hidden
        gate[at] = sig * (1.0 + pre * (1.0 - sig))
        values[at] = dot(hidden, w_out_ref[...]).astype(BF16)
        for k, (mine, out) in enumerate(((feats, feats_ref), (act, act_ref), (gate, gate_ref))):
            copy(mine.at[at], out.at[at], out_sems.at[k]).start()
        return carry

    lax.fori_loop(0, acc.shape[0] // chunk, body, 0)
    spread(recv_ref, mask, sems.at[2], mask_ref, values, made, out_ref, out_sems.at[3])
    for k, (mine, out) in enumerate(((feats, feats_ref), (act, act_ref), (gate, gate_ref), (made, out_ref))):
        copy(mine, out, out_sems.at[k]).wait()


def backward_kernel(
    recv_ref, arrived_ref, mask_t_ref, mask_ref, scale_ref, w_in_ref, w_out_ref,
    feats_ref, act_ref, gate_ref, out_ref, grads,
    arrived, mask_t, mask, made, acc, values, feats, act, gate, sems, in_sems,
):
    width, inner = feats.shape[1], act.shape[1]
    per = 2 * STEP_OWNERS
    start_all(arrived_ref, arrived, sems.at[0], STEP_OWNERS)
    start_all(mask_t_ref, mask_t, sems.at[1], per)
    kept = ((feats_ref, feats), (act_ref, act), (gate_ref, gate))
    for k, (src, dst) in enumerate(kept):
        copy(src, dst, in_sems.at[k]).start()
    start_all(mask_ref, mask, sems.at[2], per)
    acc[...] = jnp.zeros_like(acc)
    grads[...] = jnp.zeros_like(grads)
    collect(recv_ref, arrived, mask_t, sems.at[0], sems.at[1], arrived_ref, mask_t_ref, acc)
    for k, (src, dst) in enumerate(kept):
        copy(src, dst, in_sems.at[k]).wait()
    chunk = 256

    def body(i, carry):
        at = pl.ds(pl.multiple_of(i * chunk, chunk), chunk)
        d_edge = acc[at].astype(BF16)
        d_act = dot(d_edge, w_out_ref[...], ((1,), (1,)))
        d_pre = (d_act * gate[at]).astype(BF16)
        values[at] = (dot(d_pre, w_in_ref[...], ((1,), (1,))) * scale_ref[at]).astype(BF16)
        grads[:inner] += dot(act[at], d_edge, ((0,), (0,)))
        in_part = dot(feats[at], d_pre, ((0,), (0,)))
        for piece in range(inner // width):
            first = inner + piece * width
            grads[first : first + width] += in_part[:, piece * width : (piece + 1) * width]
        return carry

    lax.fori_loop(0, acc.shape[0] // chunk, body, 0)
    spread(recv_ref, mask, sems.at[2], mask_ref, values, made, out_ref, in_sems.at[3])
    copy(made, out_ref, in_sems.at[3]).wait()


def edge_scratch(owners, edges, width, inner):
    tiles = 2 * owners
    steps = owners // STEP_OWNERS
    return [
        pltpu.VMEM((owners, 2 * TILE, width), BF16),
        pltpu.VMEM((tiles, TILE, TILE), BF16),
        pltpu.VMEM((tiles, TILE, TILE), BF16),
        pltpu.VMEM((owners, 2 * TILE, width), BF16),
        pltpu.VMEM((edges, width), F32),
        pltpu.VMEM((edges, width), BF16),
        pltpu.VMEM((edges, width), BF16),
        pltpu.VMEM((edges, inner), BF16),
        pltpu.VMEM((edges, inner), F32),
    ], [pltpu.SemaphoreType.DMA((3, steps)), pltpu.SemaphoreType.DMA((4,))]


def edges_forward(recv, arrived, mask_t, mask, scale, w_in, w_out):
    owners = arrived.shape[0]
    edges, width, inner = scale.shape[0], w_in.shape[0], w_in.shape[1]
    buffers, sems = edge_scratch(owners, edges, width, inner)
    return pl.pallas_call(
        forward_kernel,
        out_shape=(
            jax.ShapeDtypeStruct((owners, 2 * TILE, width), BF16),
            jax.ShapeDtypeStruct((edges, width), BF16),
            jax.ShapeDtypeStruct((edges, inner), BF16),
            jax.ShapeDtypeStruct((edges, inner), F32),
        ),
        in_specs=[SMEM, ANY, ANY, ANY, VMEM, VMEM, VMEM],
        out_specs=(ANY,) * 4,
        scratch_shapes=buffers + sems,
        compiler_params=PARAMS,
        name="edges_forward",
    )(recv, arrived, mask_t, mask, scale, w_in, w_out)


def edges_backward(recv, arrived, mask_t, mask, scale, w_in, w_out, feats, act, gate):
    owners = arrived.shape[0]
    edges, width, inner = scale.shape[0], w_in.shape[0], w_in.shape[1]
    buffers, sems = edge_scratch(owners, edges, width, inner)
    return pl.pallas_call(
        backward_kernel,
        out_shape=(
            jax.ShapeDtypeStruct((owners, 2 * TILE, width), BF16),
            jax.ShapeDtypeStruct((2 * inner, width), F32),
        ),
        in_specs=[SMEM, ANY, ANY, ANY, VMEM, VMEM, VMEM, ANY, ANY, ANY],
        out_specs=(ANY, VMEM),
        scratch_shapes=buffers + sems,
        compiler_params=PARAMS,
        name="edges_backward",
    )(recv, arrived, mask_t, mask, scale, w_in, w_out, feats, act, gate)


def gather_sum_kernel(send_ref, arrived_ref, out_ref, arrived, sems):
    per = 2 * STEP_OWNERS
    start_all(arrived_ref, arrived, sems, STEP_OWNERS)
    out_ref[...] = jnp.zeros_like(out_ref)

    def body(i, carry):
        copy(part(arrived_ref, i, STEP_OWNERS), part(arrived, i, STEP_OWNERS), sems.at[i]).wait()
        for tile in range(per):
            where = rows_at(send_ref[i * per + tile])
            rows = arrived[i * STEP_OWNERS + tile // 2, tile % 2 * TILE : (tile % 2 + 1) * TILE]
            out_ref[where] += rows.astype(F32)
        return carry

    lax.fori_loop(0, arrived.shape[0] // STEP_OWNERS, body, 0)


def gather_sum(send, arrived, nodes):
    owners, _, width = arrived.shape
    return pl.pallas_call(
        gather_sum_kernel,
        out_shape=jax.ShapeDtypeStruct((nodes, width), F32),
        in_specs=[SMEM, ANY],
        out_specs=VMEM,
        scratch_shapes=[
            pltpu.VMEM((owners, 2 * TILE, width), BF16),
            pltpu.SemaphoreType.DMA((owners // STEP_OWNERS,)),
        ],
        compiler_params=PARAMS,
        name="node_sums",
    )(send, arrived)


def norm_kernel(
    send_ref, mine_ref, other_ref, feats_ref, cot_ref, gain_ref, updated_ref, part_ref, out_ref, d_summed, sem
):
    gain = gain_ref[...]

    def body(i, part):
        at = rows_at(i)
        summed = mine_ref[at] + other_ref[at]
        inv_rms = lax.rsqrt(jnp.mean(summed * summed, axis=-1, keepdims=True) + 1e-05)
        normed = summed * inv_rms
        updated_ref[at] = (feats_ref[at].astype(F32) + normed * gain).astype(BF16)
        upstream = cot_ref[at].astype(F32)
        d_normed = upstream * gain
        inner = jnp.mean(d_normed * normed, axis=-1, keepdims=True)
        d_summed[at] = (inv_rms * (d_normed - normed * inner)).astype(BF16)
        return part + jnp.sum((upstream * normed).reshape(TILE // 8, 8, -1), axis=0)

    part_ref[...] = lax.fori_loop(0, mine_ref.shape[0] // TILE, body, jnp.zeros_like(part_ref))
    send_blocks(send_ref, d_summed, out_ref, sem)


def norm_and_select(send, mine, other, feats, cot, gain, owners):
    nodes, width = feats.shape
    updated, gain_part, out = pl.pallas_call(
        norm_kernel,
        out_shape=(
            jax.ShapeDtypeStruct((nodes, width), BF16),
            jax.ShapeDtypeStruct((8, width), F32),
            jax.ShapeDtypeStruct((2 * owners, TILE, width), BF16),
        ),
        in_specs=[SMEM] + [VMEM] * 5,
        out_specs=(VMEM, VMEM, ANY),
        scratch_shapes=[pltpu.VMEM((nodes, width), BF16), pltpu.SemaphoreType.DMA],
        compiler_params=PARAMS,
        name="norm_and_select",
    )(send, mine, other, feats, cot, gain)
    return updated, gain_part, out.reshape(owners, 2 * TILE, width)


def exchange(rows):
    owners, width = rows.shape[0], rows.shape[2]
    tiles = rows.reshape(2 * owners, TILE, width)
    moved = lax.all_to_all(tiles, ("wide", "narrow"), split_axis=0, concat_axis=0, tiled=True)
    return moved.reshape(owners, 2 * TILE, width)


def swap(rows):
    return lax.ppermute(rows, "narrow", [(0, 1), (1, 0)])


def ring_sends(values, stride, side):
    owners = lax.axis_size("wide")
    moved = []
    for offset in range(1, side):
        pairs = []
        for w in range(owners):
            place = w // stride % side
            pairs.append((w, w + ((place + offset) % side - place) * stride))
        moved.append(lax.ppermute(values[offset - 1], "wide", pairs))
    return moved


def axes_of(owners):
    side = 4
    strides = []
    stride = owners // side
    while stride >= 1:
        strides.append(stride)
        stride //= side
    return side, strides


def reduce_over_chips(rows):
    core = lax.axis_index("narrow")
    wide = lax.axis_index("wide")
    side, strides = axes_of(lax.axis_size("wide"))
    half = rows.shape[0] // 2
    theirs = swap(lax.dynamic_slice_in_dim(rows, (1 - core) * half, half, 0))
    held = lax.dynamic_slice_in_dim(rows, core * half, half, 0) + theirs
    for stride in strides:
        place = wide // stride % side
        pieces = held.reshape((side, -1) + held.shape[1:])
        pick = lambda o: lax.dynamic_index_in_dim(pieces, (place + o) % side, 0, keepdims=False)
        moved = ring_sends([pick(o) for o in range(1, side)], stride, side)
        held = pick(0) + moved[0] + moved[1] + moved[2]
    for stride in reversed(strides):
        held = in_order([held] + ring_sends([held] * (side - 1), stride, side), wide // stride % side)
        held = held.reshape((-1,) + held.shape[2:])
    other = swap(held)
    first, second = jnp.where(core == 0, held, other), jnp.where(core == 0, other, held)
    return jnp.concatenate([first, second], 0)


def in_order(pieces, place):
    side = len(pieces)
    return jnp.take(jnp.stack(pieces), (place - jnp.arange(side)) % side, axis=0)


def sum_over_wide(row):
    wide = lax.axis_index("wide")
    side, strides = axes_of(lax.axis_size("wide"))
    for stride in strides:
        row = in_order([row] + ring_sends([row] * (side - 1), stride, side), wide // stride % side).sum(0)
    return row


def shards(
    node_feats,
    send_block,
    recv_block,
    tile_count,
    mask_bits,
    degree,
    weight_in,
    weight_out,
    norm_gain,
    cotangent,
):
    owners = lax.axis_size("wide")
    nodes, width = node_feats.shape
    inner = weight_in.shape[1]
    core = lax.axis_index("narrow")
    my_slots = send_block[0, :, 0, :]
    own = lax.dynamic_index_in_dim(my_slots, core, 1, keepdims=False)
    theirs = swap(lax.dynamic_index_in_dim(my_slots, 1 - core, 1, keepdims=False))
    send = jnp.where(core == 0, jnp.stack([own, theirs], 1), jnp.stack([theirs, own], 1)).reshape(-1)
    recv = recv_block.reshape(-1)
    count = tile_count.reshape(-1)
    words = mask_bits.reshape((-1,) + mask_bits.shape[4:])
    scale = lax.rsqrt(degree.astype(F32))[:, None]
    gain = norm_gain[None, :]

    mask, mask_t = unpack(count, words)
    arrived = exchange(select(send, node_feats, owners))
    products, feats, act, gate = edges_forward(recv, arrived, mask_t, mask, scale, weight_in, weight_out)
    mine = gather_sum(send, exchange(products), nodes)
    updated, gain_part, picked = norm_and_select(send, mine, swap(mine), node_feats, cotangent, gain, owners)
    products, grads = edges_backward(
        recv, exchange(picked), mask_t, mask, scale, weight_in, weight_out, feats, act, gate
    )
    arrived = exchange(products)
    grads, gain_part = lax.optimization_barrier((grads, gain_part))
    grad_gain = sum_over_wide(gain_part.sum(0).reshape(-1, width // 2)).reshape(width)
    grads = reduce_over_chips(grads)
    mine = gather_sum(send, arrived, nodes)
    grad_nodes = cotangent.astype(F32) + (mine + swap(mine))
    pieces = inner // width
    grad_out = grads[:inner]
    grad_in = grads[inner:].reshape(pieces, width, width).transpose(1, 0, 2).reshape(width, inner)

    edge_factor = (degree.shape[0] * owners * lax.axis_size("narrow")) ** (-0.5)
    return (
        updated,
        grad_nodes,
        grad_in * edge_factor,
        grad_out * edge_factor,
        grad_gain * (nodes * owners) ** (-0.5),
    )


def solution(mesh):
    return jax.shard_map(
        shards,
        mesh=mesh,
        in_specs=(
            P("wide", None),
            P("wide", None, "narrow", None),
            P("wide", "narrow", None, None),
            P("wide", "narrow", None),
            P("wide", "narrow", None, None, None, None),
            P(("wide", "narrow")),
            P(),
            P(),
            P(),
            P("wide", None),
        ),
        out_specs=(P("wide", None), P("wide", None), P(), P(), P()),
        check_vma=False,
    )
```

```python
import functools

import jax
import jax.numpy as jnp
from jax import lax
from jax.experimental import pallas as pl
from jax.experimental.pallas import tpu as pltpu
from jax.sharding import PartitionSpec as P

F32 = jnp.float32
BF16 = jnp.bfloat16
TILE = 128
LANES = 128
STEP_OWNERS = 4
PARAMS = pltpu.CompilerParams(vmem_limit_bytes=52 * 1024 * 1024)


SMEM = pl.BlockSpec(memory_space=pltpu.SMEM)
VMEM = pl.BlockSpec(memory_space=pltpu.VMEM)
ANY = pl.BlockSpec(memory_space=pl.ANY)


def dot(a, b, dims=((1,), (0,))):
    return lax.dot_general(a, b, (dims, ((), ())), preferred_element_type=F32)


def rows_at(block):
    return pl.ds(pl.multiple_of(block * TILE, TILE), TILE)


def unpack_kernel(count_ref, words_ref, bit_ref, mask_ref, mask_t_ref):
    step = pl.program_id(0)
    tiles = words_ref.shape[0]
    row = lax.broadcasted_iota(jnp.int32, (8, TILE), 0)
    for tile in range(tiles):
        slot = tile % 2
        live = count_ref[step * (tiles // 2) + tile // 2] > slot
        words = jnp.where(live, words_ref[tile], 0)
        groups = []
        for first in range(0, TILE, 8):
            low, high = first // 15, (first + 7) // 15
            picked = jnp.broadcast_to(words[low : low + 1], (8, TILE))
            if high != low:
                later = jnp.broadcast_to(words[high : high + 1], (8, TILE))
                picked = jnp.where(row + first >= high * 15, later, picked)
            hit = jnp.bitwise_and(picked, bit_ref[first : first + 8]) != 0
            groups.append(jnp.where(hit, 1.0, 0.0).astype(F32))
        mask = jnp.concatenate(groups, axis=0)
        mask_ref[tile] = mask.astype(BF16)
        mask_t_ref[tile] = mask.T.astype(BF16)


def unpack(count, words):
    tiles = words.shape[0]
    per = 8
    bit = jnp.left_shift(1, lax.broadcasted_iota(jnp.int32, (TILE, TILE), 0) % 15)
    out = jax.ShapeDtypeStruct((tiles, TILE, TILE), BF16)
    block = pl.BlockSpec((per, TILE, TILE), lambda i, c: (i, 0, 0))
    return pl.pallas_call(
        unpack_kernel,
        out_shape=(out, out),
        grid_spec=pltpu.PrefetchScalarGridSpec(
            num_scalar_prefetch=1,
            grid=(tiles // per,),
            in_specs=[
                pl.BlockSpec((per,) + words.shape[1:], lambda i, c: (i, 0, 0)),
                pl.BlockSpec((TILE, TILE), lambda i, c: (0, 0)),
            ],
            out_specs=(block, block),
        ),
        compiler_params=PARAMS,
        cost_estimate=pl.CostEstimate(flops=tiles * 2**18, bytes_accessed=tiles * 2**17, transcendentals=0),
        name="unpack_masks",
    )(count, words, bit)


def copy(src, dst, sem):
    return pltpu.make_async_copy(src, dst, sem)


def send_blocks(send_ref, rows_ref, out_ref, sem):
    def body(i, carry):
        copy(rows_ref.at[rows_at(send_ref[i])], out_ref.at[i], sem).start()
        return carry

    lax.fori_loop(0, out_ref.shape[0], body, 0, unroll=8)
    copy(out_ref, out_ref, sem).wait()


def select(send, rows, owners):
    tiles, features = 2 * owners, rows.shape[1]
    out = pl.pallas_call(
        send_blocks,
        out_shape=jax.ShapeDtypeStruct((tiles, TILE, features), BF16),
        in_specs=[SMEM, VMEM],
        out_specs=ANY,
        scratch_shapes=[pltpu.SemaphoreType.DMA],
        compiler_params=PARAMS,
        name="select_blocks",
    )(send, rows)
    return out


def part(ref, i, size):
    return ref.at[pl.ds(i * size, size)]


def start_all(src, dst, sems, size):
    def body(i, carry):
        copy(part(src, i, size), part(dst, i, size), sems.at[i]).start()
        return carry

    lax.fori_loop(0, src.shape[0] // size, body, 0)


def collect(recv_ref, arrived, mask_t, arrived_sems, mask_sems, arrived_ref, mask_t_ref, acc):
    per = 2 * STEP_OWNERS

    def body(i, carry):
        copy(part(arrived_ref, i, STEP_OWNERS), part(arrived, i, STEP_OWNERS), arrived_sems.at[i]).wait()
        copy(part(mask_t_ref, i, per), part(mask_t, i, per), mask_sems.at[i]).wait()
        for tile in range(per):
            where = rows_at(recv_ref[i * per + tile])
            rows = arrived[i * STEP_OWNERS + tile // 2, tile % 2 * TILE : (tile % 2 + 1) * TILE]
            acc[where] += dot(mask_t[i * per + tile], rows)
        return carry

    lax.fori_loop(0, arrived.shape[0] // STEP_OWNERS, body, 0)


def spread(recv_ref, mask, mask_sems, mask_ref, values, made, out_ref, sem, grads=None):
    per = 2 * STEP_OWNERS

    def body(i, carry):
        copy(part(mask_ref, i, per), part(mask, i, per), mask_sems.at[i]).wait()
        for tile in range(per):
            where = rows_at(recv_ref[i * per + tile])
            product = dot(mask[i * per + tile], values[where]).astype(BF16)
            for h in range(product.shape[1] // LANES):
                made[i * per + tile, h * TILE : (h + 1) * TILE] = product[:, h * LANES : (h + 1) * LANES]
            if grads is not None:
                first = product.shape[1] // LANES * TILE
                extra = made.shape[1] - first
                at = pl.ds(pl.multiple_of((i * per + tile) * extra, extra), extra)
                made[i * per + tile, first:] = grads[at].astype(BF16)
        copy(part(made, i, per), part(out_ref, i, per), sem).start()
        return carry

    lax.fori_loop(0, made.shape[0] // per, body, 0)


def forward_kernel(
    recv_ref, arrived_ref, mask_t_ref, mask_ref, scale_ref, w_in_ref, w_out_ref,
    out_ref, feats_ref, act_ref, gate_ref,
    arrived, mask_t, mask, made, acc, values, feats, act, gate, sems, out_sems,
):
    per = 2 * STEP_OWNERS
    start_all(arrived_ref, arrived, sems.at[0], STEP_OWNERS)
    start_all(mask_t_ref, mask_t, sems.at[1], per)
    start_all(mask_ref, mask, sems.at[2], per)
    acc[...] = jnp.zeros_like(acc)
    collect(recv_ref, arrived, mask_t, sems.at[0], sems.at[1], arrived_ref, mask_t_ref, acc)
    chunk = 256

    def body(i, carry):
        at = pl.ds(pl.multiple_of(i * chunk, chunk), chunk)
        rows = (acc[at] * scale_ref[at]).astype(BF16)
        feats[at] = rows
        pre = dot(rows, w_in_ref[...])
        sig = jax.nn.sigmoid(pre)
        hidden = (pre * sig).astype(BF16)
        act[at] = hidden
        gate[at] = sig * (1.0 + pre * (1.0 - sig))
        values[at] = dot(hidden, w_out_ref[...]).astype(BF16)
        for k, (mine, out) in enumerate(((feats, feats_ref), (act, act_ref), (gate, gate_ref))):
            copy(mine.at[at], out.at[at], out_sems.at[k]).start()
        return carry

    lax.fori_loop(0, acc.shape[0] // chunk, body, 0)
    spread(recv_ref, mask, sems.at[2], mask_ref, values, made, out_ref, out_sems.at[3])
    for k, (mine, out) in enumerate(((feats, feats_ref), (act, act_ref), (gate, gate_ref), (made, out_ref))):
        copy(mine, out, out_sems.at[k]).wait()


def backward_kernel(
    recv_ref, arrived_ref, mask_t_ref, mask_ref, scale_ref, w_in_ref, w_out_ref,
    feats_ref, act_ref, gate_ref, out_ref,
    arrived, mask_t, mask, made, acc, values, feats, act, gate, grads, sems, in_sems,
):
    width, inner = feats.shape[1], act.shape[1]
    per = 2 * STEP_OWNERS
    start_all(arrived_ref, arrived, sems.at[0], STEP_OWNERS)
    start_all(mask_t_ref, mask_t, sems.at[1], per)
    kept = ((feats_ref, feats), (act_ref, act), (gate_ref, gate))
    for k, (src, dst) in enumerate(kept):
        copy(src, dst, in_sems.at[k]).start()
    start_all(mask_ref, mask, sems.at[2], per)
    acc[...] = jnp.zeros_like(acc)
    grads[...] = jnp.zeros_like(grads)
    collect(recv_ref, arrived, mask_t, sems.at[0], sems.at[1], arrived_ref, mask_t_ref, acc)
    for k, (src, dst) in enumerate(kept):
        copy(src, dst, in_sems.at[k]).wait()
    chunk = 256

    def body(i, carry):
        at = pl.ds(pl.multiple_of(i * chunk, chunk), chunk)
        d_edge = acc[at].astype(BF16)
        d_act = dot(d_edge, w_out_ref[...], ((1,), (1,)))
        d_pre = (d_act * gate[at]).astype(BF16)
        values[at] = (dot(d_pre, w_in_ref[...], ((1,), (1,))) * scale_ref[at]).astype(BF16)
        first = 0
        for grad in (dot(act[at], d_edge, ((0,), (0,))), dot(feats[at], d_pre, ((0,), (0,)))):
            for lane in range(0, grad.shape[1], LANES):
                grads[first : first + grad.shape[0]] += grad[:, lane : lane + LANES]
                first += grad.shape[0]
        return carry

    lax.fori_loop(0, acc.shape[0] // chunk, body, 0)
    spread(recv_ref, mask, sems.at[2], mask_ref, values, made, out_ref, in_sems.at[3], grads)
    copy(made, out_ref, in_sems.at[3]).wait()


def edge_scratch(owners, rows, edges, width, inner):
    tiles = 2 * owners
    steps = owners // STEP_OWNERS
    return [
        pltpu.VMEM((owners, 2 * TILE, width), BF16),
        pltpu.VMEM((tiles, TILE, TILE), BF16),
        pltpu.VMEM((tiles, TILE, TILE), BF16),
        pltpu.VMEM((tiles, rows, LANES), BF16),
        pltpu.VMEM((edges, width), F32),
        pltpu.VMEM((edges, width), BF16),
        pltpu.VMEM((edges, width), BF16),
        pltpu.VMEM((edges, inner), BF16),
        pltpu.VMEM((edges, inner), F32),
    ], [pltpu.SemaphoreType.DMA((3, steps)), pltpu.SemaphoreType.DMA((4,))]


def edges_forward(recv, arrived, mask_t, mask, scale, w_in, w_out):
    owners = arrived.shape[0]
    edges, width, inner = scale.shape[0], w_in.shape[0], w_in.shape[1]
    rows = width // LANES * TILE
    buffers, sems = edge_scratch(owners, rows, edges, width, inner)
    return pl.pallas_call(
        forward_kernel,
        out_shape=(
            jax.ShapeDtypeStruct((2 * owners, rows, LANES), BF16),
            jax.ShapeDtypeStruct((edges, width), BF16),
            jax.ShapeDtypeStruct((edges, inner), BF16),
            jax.ShapeDtypeStruct((edges, inner), F32),
        ),
        in_specs=[SMEM, ANY, ANY, ANY, VMEM, VMEM, VMEM],
        out_specs=(ANY,) * 4,
        scratch_shapes=buffers + sems,
        compiler_params=PARAMS,
        name="edges_forward",
    )(recv, arrived, mask_t, mask, scale, w_in, w_out)


def edges_backward(recv, arrived, mask_t, mask, scale, w_in, w_out, feats, act, gate):
    owners = arrived.shape[0]
    edges, width, inner = scale.shape[0], w_in.shape[0], w_in.shape[1]
    grad_rows = 2 * inner * width // LANES
    rows = width // LANES * TILE + grad_rows // (2 * owners)
    buffers, sems = edge_scratch(owners, rows, edges, width, inner)
    return pl.pallas_call(
        backward_kernel,
        out_shape=jax.ShapeDtypeStruct((2 * owners, rows, LANES), BF16),
        in_specs=[SMEM, ANY, ANY, ANY, VMEM, VMEM, VMEM, ANY, ANY, ANY],
        out_specs=ANY,
        scratch_shapes=buffers + [pltpu.VMEM((grad_rows, LANES), F32)] + sems,
        compiler_params=PARAMS,
        name="edges_backward",
    )(recv, arrived, mask_t, mask, scale, w_in, w_out, feats, act, gate)


def gather_sum_kernel(send_ref, arrived_ref, out_ref, arrived, sems):
    per = 2 * STEP_OWNERS
    start_all(arrived_ref, arrived, sems, per)
    out_ref[...] = jnp.zeros_like(out_ref)

    def body(i, carry):
        copy(part(arrived_ref, i, per), part(arrived, i, per), sems.at[i]).wait()
        for tile in range(per):
            where = rows_at(send_ref[i * per + tile])
            for h in range(out_ref.shape[1] // LANES):
                rows = arrived[i * per + tile, h * TILE : (h + 1) * TILE]
                out_ref[where, h * LANES : (h + 1) * LANES] += rows.astype(F32)
        return carry

    lax.fori_loop(0, arrived.shape[0] // per, body, 0)


def gather_sum(send, arrived, nodes, width):
    return pl.pallas_call(
        gather_sum_kernel,
        out_shape=jax.ShapeDtypeStruct((nodes, width), F32),
        in_specs=[SMEM, ANY],
        out_specs=VMEM,
        scratch_shapes=[
            pltpu.VMEM(arrived.shape, BF16),
            pltpu.SemaphoreType.DMA((arrived.shape[0] // (2 * STEP_OWNERS),)),
        ],
        compiler_params=PARAMS,
        name="node_sums",
    )(send, arrived)


def tail_sum_kernel(arrived_ref, out_ref, tails, sem):
    first = arrived_ref.shape[1] - tails.shape[1]
    move = copy(arrived_ref.at[:, pl.ds(first, tails.shape[1])], tails, sem)
    move.start()
    move.wait()
    out_ref[...] = jnp.sum(tails[...].astype(F32), axis=0)


def tail_sum(arrived, rows):
    tiles, total, lanes = arrived.shape
    return pl.pallas_call(
        tail_sum_kernel,
        out_shape=jax.ShapeDtypeStruct((total - rows, lanes), F32),
        in_specs=[ANY],
        out_specs=VMEM,
        scratch_shapes=[pltpu.VMEM((tiles, total - rows, lanes), BF16), pltpu.SemaphoreType.DMA],
        compiler_params=PARAMS,
        name="weight_sums",
    )(arrived)


def norm_kernel(
    send_ref, mine_ref, other_ref, feats_ref, cot_ref, gain_ref, updated_ref, part_ref, out_ref, d_summed, sem
):
    gain = gain_ref[...]

    def body(i, part):
        at = rows_at(i)
        summed = mine_ref[at] + other_ref[at]
        inv_rms = lax.rsqrt(jnp.mean(summed * summed, axis=-1, keepdims=True) + 1e-05)
        normed = summed * inv_rms
        updated_ref[at] = (feats_ref[at].astype(F32) + normed * gain).astype(BF16)
        upstream = cot_ref[at].astype(F32)
        d_normed = upstream * gain
        inner = jnp.mean(d_normed * normed, axis=-1, keepdims=True)
        d_summed[at] = (inv_rms * (d_normed - normed * inner)).astype(BF16)
        return part + jnp.sum((upstream * normed).reshape(TILE // 8, 8, -1), axis=0)

    part_ref[...] = lax.fori_loop(0, mine_ref.shape[0] // TILE, body, jnp.zeros_like(part_ref))
    send_blocks(send_ref, d_summed, out_ref, sem)


def norm_and_select(send, mine, other, feats, cot, gain, owners):
    nodes, width = feats.shape
    updated, gain_part, out = pl.pallas_call(
        norm_kernel,
        out_shape=(
            jax.ShapeDtypeStruct((nodes, width), BF16),
            jax.ShapeDtypeStruct((8, width), F32),
            jax.ShapeDtypeStruct((2 * owners, TILE, width), BF16),
        ),
        in_specs=[SMEM] + [VMEM] * 5,
        out_specs=(VMEM, VMEM, ANY),
        scratch_shapes=[pltpu.VMEM((nodes, width), BF16), pltpu.SemaphoreType.DMA],
        compiler_params=PARAMS,
        name="norm_and_select",
    )(send, mine, other, feats, cot, gain)
    return updated, gain_part, out


def exchange(tiles):
    return lax.all_to_all(tiles, ("wide", "narrow"), split_axis=0, concat_axis=0, tiled=True)


def swap(rows):
    return lax.ppermute(rows, "narrow", [(0, 1), (1, 0)])


def shards(
    node_feats,
    send_block,
    recv_block,
    tile_count,
    mask_bits,
    degree,
    weight_in,
    weight_out,
    norm_gain,
    cotangent,
):
    owners = lax.axis_size("wide")
    nodes, width = node_feats.shape
    inner = weight_in.shape[1]
    core = lax.axis_index("narrow")
    my_slots = send_block[0, :, 0, :]
    own = lax.dynamic_index_in_dim(my_slots, core, 1, keepdims=False)
    theirs = swap(lax.dynamic_index_in_dim(my_slots, 1 - core, 1, keepdims=False))
    send = jnp.where(core == 0, jnp.stack([own, theirs], 1), jnp.stack([theirs, own], 1)).reshape(-1)
    recv = recv_block.reshape(-1)
    count = tile_count.reshape(-1)
    words = mask_bits.reshape((-1,) + mask_bits.shape[4:])
    scale = lax.rsqrt(degree.astype(F32))[:, None]
    gain = norm_gain[None, :]

    mask, mask_t = unpack(count, words)
    by_owner = lambda tiles: tiles.reshape(owners, 2 * TILE, width)
    arrived = by_owner(exchange(select(send, node_feats, owners)))
    products, feats, act, gate = edges_forward(recv, arrived, mask_t, mask, scale, weight_in, weight_out)
    mine = gather_sum(send, exchange(products), nodes, width)
    updated, gain_part, picked = norm_and_select(send, mine, swap(mine), node_feats, cotangent, gain, owners)
    arrived = by_owner(exchange(picked))
    products = edges_backward(recv, arrived, mask_t, mask, scale, weight_in, weight_out, feats, act, gate)
    arrived = exchange(products)

    weight_sums = tail_sum(arrived, width // LANES * TILE)
    extra = weight_sums.shape[0]
    chunk = jnp.concatenate([weight_sums, gain_part.sum(0).reshape(-1, LANES)], 0)
    chunk = jnp.pad(chunk, ((0, -chunk.shape[0] % 8), (0, 0)))
    everyone = lax.all_to_all(
        jnp.broadcast_to(chunk[None], (owners,) + chunk.shape), "wide", split_axis=0, concat_axis=0, tiled=True
    )
    mine = gather_sum(send, arrived, nodes, width)
    grad_nodes = cotangent.astype(F32) + (mine + swap(mine))

    grad_gain = everyone[:, extra : extra + width // LANES].sum(0).reshape(width)
    held = everyone[:, :extra]
    theirs = swap(held)
    grads = jnp.stack([jnp.where(core == 0, held, theirs), jnp.where(core == 0, theirs, held)], 1)
    grads = grads.reshape(-1, LANES)
    grad_out = jnp.concatenate(jnp.split(grads[: inner * width // LANES], width // LANES), 1)
    grad_in = jnp.concatenate(jnp.split(grads[inner * width // LANES :], inner // LANES), 1)

    edge_factor = (degree.shape[0] * owners * lax.axis_size("narrow")) ** (-0.5)
    return (
        updated,
        grad_nodes,
        grad_in * edge_factor,
        grad_out * edge_factor,
        grad_gain * (nodes * owners) ** (-0.5),
    )


def solution(mesh):
    return jax.shard_map(
        shards,
        mesh=mesh,
        in_specs=(
            P("wide", None),
            P("wide", None, "narrow", None),
            P("wide", "narrow", None, None),
            P("wide", "narrow", None),
            P("wide", "narrow", None, None, None, None),
            P(("wide", "narrow")),
            P(),
            P(),
            P(),
            P("wide", None),
        ),
        out_specs=(P("wide", None), P("wide", None), P(), P(), P()),
        check_vma=False,
    )
```

```python
import functools

import jax
import jax.numpy as jnp
from jax import lax
from jax.experimental import pallas as pl
from jax.experimental.pallas import tpu as pltpu
from jax.sharding import PartitionSpec as P

F32 = jnp.float32
BF16 = jnp.bfloat16
TILE = 128
LANES = 128
STEP_TILES = 8
PARAMS = pltpu.CompilerParams(vmem_limit_bytes=12 * 1024 * 1024)


SMEM = pl.BlockSpec(memory_space=pltpu.SMEM)
VMEM = pl.BlockSpec(memory_space=pltpu.VMEM)


def dot(a, b, dims=((1,), (0,))):
    return lax.dot_general(a, b, (dims, ((), ())), preferred_element_type=F32)


def rows_at(block):
    return pl.ds(pl.multiple_of(block * TILE, TILE), TILE)


def unpack_kernel(count_ref, words_ref, mask_ref, mask_t_ref):
    step = pl.program_id(0)
    owners, words, slots, _ = words_ref.shape
    row = lax.broadcasted_iota(jnp.int32, (8, TILE), 0)
    for owner in range(owners):
        count = count_ref[step * owners + owner]
        for slot in range(slots):
            live = jnp.where(count > slot, jnp.int32(-1), jnp.int32(0))
            word = [jnp.broadcast_to(words_ref[owner, j, slot : slot + 1], (8, TILE)) & live for j in range(words)]
            groups = []
            for first in range(0, TILE, 8):
                low, high = first // 15, (first + 7) // 15
                picked = word[low]
                shift = row + (first - low * 15)
                if high != low:
                    later = row >= high * 15 - first
                    picked = jnp.where(later, word[high], picked)
                    shift = jnp.where(later, shift - 15, shift)
                groups.append((jnp.right_shift(picked, shift) & 1).astype(F32))
            mask = jnp.concatenate(groups, axis=0)
            mask_ref[owner * slots + slot] = mask.astype(BF16)
            mask_t_ref[owner * slots + slot] = mask.T.astype(BF16)


def unpack(count, words):
    owners, _, slots, _ = words.shape
    per = 8
    out = jax.ShapeDtypeStruct((owners * slots, TILE, TILE), BF16)
    block = pl.BlockSpec((per * slots, TILE, TILE), lambda i, c: (i, 0, 0))
    return pl.pallas_call(
        unpack_kernel,
        out_shape=(out, out),
        grid_spec=pltpu.PrefetchScalarGridSpec(
            num_scalar_prefetch=1,
            grid=(owners // per,),
            in_specs=[pl.BlockSpec((per,) + words.shape[1:], lambda i, c: (i, 0, 0, 0))],
            out_specs=(block, block),
        ),
        compiler_params=PARAMS,
        name="unpack_masks",
    )(count, words)


def steps_of(tiles):
    return tiles.shape[0] // STEP_TILES


def select_kernel(send_ref, rows_ref, out_ref):
    def body(i, carry):
        for tile in range(STEP_TILES):
            out_ref[i * STEP_TILES + tile] = rows_ref[rows_at(send_ref[i * STEP_TILES + tile])]
        return carry

    lax.fori_loop(0, steps_of(out_ref), body, 0)


def select(send, rows):
    return pl.pallas_call(
        select_kernel,
        out_shape=jax.ShapeDtypeStruct((send.shape[0], TILE, rows.shape[1]), BF16),
        in_specs=[SMEM, VMEM],
        out_specs=VMEM,
        compiler_params=PARAMS,
        name="select_blocks",
    )(send, rows)


def collect(recv_ref, arrived, mask_t, acc):
    acc[...] = jnp.zeros_like(acc)

    def body(i, carry):
        for tile in range(STEP_TILES):
            where = rows_at(recv_ref[i * STEP_TILES + tile])
            acc[where] += dot(mask_t[i * STEP_TILES + tile], arrived[i * STEP_TILES + tile])
        return carry

    lax.fori_loop(0, steps_of(arrived), body, 0)


def spread(recv_ref, mask, values, made, grads=None):
    def body(i, carry):
        for tile in range(STEP_TILES):
            where = rows_at(recv_ref[i * STEP_TILES + tile])
            product = dot(mask[i * STEP_TILES + tile], values[where]).astype(BF16)
            for h in range(product.shape[1] // LANES):
                made[i * STEP_TILES + tile, h * TILE : (h + 1) * TILE] = product[:, h * LANES : (h + 1) * LANES]
            if grads is not None:
                first = product.shape[1] // LANES * TILE
                extra = made.shape[1] - first
                at = pl.ds(pl.multiple_of((i * STEP_TILES + tile) * extra, extra), extra)
                made[i * STEP_TILES + tile, first:] = grads[at].astype(BF16)
        return carry

    lax.fori_loop(0, steps_of(made), body, 0)


def scaled(rows, degree_ref, i):
    blocks = rows.shape[0] // TILE
    parts = []
    for k in range(blocks):
        scale = lax.rsqrt(degree_ref[pl.ds(i * blocks + k, 1)].astype(F32))
        scale = jnp.broadcast_to(scale, (TILE, LANES)).T
        lanes = [rows[k * TILE : (k + 1) * TILE, j : j + LANES] * scale for j in range(0, rows.shape[1], LANES)]
        parts.append(jnp.concatenate(lanes, axis=1))
    return jnp.concatenate(parts, axis=0)


def forward_kernel(
    recv_ref, arrived, mask_t, mask, degree_ref, w_in_ref, w_out_ref, made, feats, act, gate, acc, values
):
    collect(recv_ref, arrived, mask_t, acc)
    chunk = 256

    def body(i, carry):
        at = pl.ds(pl.multiple_of(i * chunk, chunk), chunk)
        rows = scaled(acc[at], degree_ref, i).astype(BF16)
        feats[at] = rows
        pre = dot(rows, w_in_ref[...])
        sig = jax.nn.sigmoid(pre)
        hidden = (pre * sig).astype(BF16)
        act[at] = hidden
        gate[at] = sig * (1.0 + pre * (1.0 - sig))
        values[at] = dot(hidden, w_out_ref[...]).astype(BF16)
        return carry

    lax.fori_loop(0, acc.shape[0] // chunk, body, 0)
    spread(recv_ref, mask, values, made)


def backward_kernel(
    recv_ref, arrived, mask_t, mask, degree_ref, w_in_ref, w_out_ref, feats, act, gate, made, acc, values, grads
):
    grads[...] = jnp.zeros_like(grads)
    collect(recv_ref, arrived, mask_t, acc)
    chunk = 256

    def body(i, carry):
        at = pl.ds(pl.multiple_of(i * chunk, chunk), chunk)
        d_edge = acc[at].astype(BF16)
        d_act = dot(d_edge, w_out_ref[...], ((1,), (1,)))
        d_pre = (d_act * gate[at]).astype(BF16)
        values[at] = scaled(dot(d_pre, w_in_ref[...], ((1,), (1,))), degree_ref, i).astype(BF16)
        first = 0
        for grad in (dot(act[at], d_edge, ((0,), (0,))), dot(feats[at], d_pre, ((0,), (0,)))):
            for lane in range(0, grad.shape[1], LANES):
                grads[first : first + grad.shape[0]] += grad[:, lane : lane + LANES]
                first += grad.shape[0]
        return carry

    lax.fori_loop(0, acc.shape[0] // chunk, body, 0)
    spread(recv_ref, mask, values, made, grads)


def edges_forward(recv, arrived, mask_t, mask, degree, w_in, w_out):
    tiles = arrived.shape[0]
    edges, width, inner = degree.size, w_in.shape[0], w_in.shape[1]
    rows = width // LANES * TILE
    return pl.pallas_call(
        forward_kernel,
        out_shape=(
            jax.ShapeDtypeStruct((tiles, rows, LANES), BF16),
            jax.ShapeDtypeStruct((edges, width), BF16),
            jax.ShapeDtypeStruct((edges, inner), BF16),
            jax.ShapeDtypeStruct((edges, inner), F32),
        ),
        in_specs=[SMEM] + [VMEM] * 6,
        out_specs=(VMEM,) * 4,
        scratch_shapes=[
            pltpu.VMEM((edges, width), F32),
            pltpu.VMEM((edges, width), BF16),
        ],
        compiler_params=PARAMS,
        name="edges_forward",
    )(recv, arrived, mask_t, mask, degree, w_in, w_out)


def edges_backward(recv, arrived, mask_t, mask, degree, w_in, w_out, feats, act, gate):
    tiles = arrived.shape[0]
    edges, width, inner = degree.size, w_in.shape[0], w_in.shape[1]
    grad_rows = 2 * inner * width // LANES
    rows = width // LANES * TILE + grad_rows // tiles
    return pl.pallas_call(
        backward_kernel,
        out_shape=jax.ShapeDtypeStruct((tiles, rows, LANES), BF16),
        in_specs=[SMEM] + [VMEM] * 9,
        out_specs=VMEM,
        scratch_shapes=[
            pltpu.VMEM((edges, width), F32),
            pltpu.VMEM((edges, width), BF16),
            pltpu.VMEM((grad_rows, LANES), F32),
        ],
        compiler_params=PARAMS,
        name="edges_backward",
    )(recv, arrived, mask_t, mask, degree, w_in, w_out, feats, act, gate)


def gather_sum_kernel(send_ref, arrived, out_ref):
    out_ref[...] = jnp.zeros_like(out_ref)

    def body(i, carry):
        for tile in range(STEP_TILES):
            where = rows_at(send_ref[i * STEP_TILES + tile])
            for h in range(out_ref.shape[1] // LANES):
                rows = arrived[i * STEP_TILES + tile, h * TILE : (h + 1) * TILE]
                out_ref[where, h * LANES : (h + 1) * LANES] += rows.astype(F32)
        return carry

    lax.fori_loop(0, steps_of(arrived), body, 0)


def gather_sum(send, arrived, nodes, width):
    return pl.pallas_call(
        gather_sum_kernel,
        out_shape=jax.ShapeDtypeStruct((nodes, width), F32),
        in_specs=[SMEM, VMEM],
        out_specs=VMEM,
        compiler_params=PARAMS,
        name="node_sums",
    )(send, arrived)


def tail_sum_kernel(arrived_ref, out_ref):
    rows = out_ref.shape[0]
    out_ref[...] = jnp.sum(arrived_ref[:, arrived_ref.shape[1] - rows :].astype(F32), axis=0)


def tail_sum(arrived, rows):
    return pl.pallas_call(
        tail_sum_kernel,
        out_shape=jax.ShapeDtypeStruct((arrived.shape[1] - rows, arrived.shape[2]), F32),
        in_specs=[VMEM],
        out_specs=VMEM,
        compiler_params=PARAMS,
        name="weight_sums",
    )(arrived)


def norm_kernel(
    send_ref, mine_ref, other_ref, feats_ref, cot_ref, gain_ref, updated_ref, part_ref, out_ref, d_summed
):
    gain = gain_ref[...]

    def body(i, part):
        at = rows_at(i)
        summed = mine_ref[at] + other_ref[at]
        inv_rms = lax.rsqrt(jnp.mean(summed * summed, axis=-1, keepdims=True) + 1e-05)
        normed = summed * inv_rms
        updated_ref[at] = (feats_ref[at].astype(F32) + normed * gain).astype(BF16)
        upstream = cot_ref[at].astype(F32)
        d_normed = upstream * gain
        inner = jnp.mean(d_normed * normed, axis=-1, keepdims=True)
        d_summed[at] = (inv_rms * (d_normed - normed * inner)).astype(BF16)
        return part + jnp.sum((upstream * normed).reshape(TILE // 8, 8, -1), axis=0)

    parts = lax.fori_loop(0, mine_ref.shape[0] // TILE, body, jnp.zeros((8, mine_ref.shape[1]), F32))
    row = jnp.sum(parts, axis=0, keepdims=True)
    part_ref[...] = jnp.zeros_like(part_ref)
    for i in range(row.shape[1] // LANES):
        part_ref[i : i + 1] = row[:, i * LANES : (i + 1) * LANES]

    select_kernel(send_ref, d_summed, out_ref)


def norm_and_select(send, mine, other, feats, cot, gain):
    nodes, width = feats.shape
    updated, gain_part, out = pl.pallas_call(
        norm_kernel,
        out_shape=(
            jax.ShapeDtypeStruct((nodes, width), BF16),
            jax.ShapeDtypeStruct((8, LANES), F32),
            jax.ShapeDtypeStruct((send.shape[0], TILE, width), BF16),
        ),
        in_specs=[SMEM] + [VMEM] * 5,
        out_specs=(VMEM,) * 3,
        scratch_shapes=[pltpu.VMEM((nodes, width), BF16)],
        compiler_params=PARAMS,
        name="norm_and_select",
    )(send, mine, other, feats, cot, gain)
    return updated, gain_part, out


def exchange(tiles):
    return lax.all_to_all(tiles, ("wide", "narrow"), split_axis=0, concat_axis=0, tiled=True)


def swap(rows):
    return lax.ppermute(rows, "narrow", [(0, 1), (1, 0)])


def shards(
    node_feats,
    send_block,
    recv_block,
    tile_count,
    mask_bits,
    degree,
    weight_in,
    weight_out,
    norm_gain,
    cotangent,
):
    owners = lax.axis_size("wide")
    nodes, width = node_feats.shape
    inner = weight_in.shape[1]
    core = lax.axis_index("narrow")
    my_slots = send_block[0, :, 0, :]
    own = lax.dynamic_index_in_dim(my_slots, core, 1, keepdims=False)
    theirs = swap(lax.dynamic_index_in_dim(my_slots, 1 - core, 1, keepdims=False))
    send = jnp.where(core == 0, jnp.stack([own, theirs], 1), jnp.stack([theirs, own], 1)).reshape(-1)
    recv = recv_block.reshape(-1)
    count = tile_count.reshape(-1)
    words = mask_bits[0, 0].transpose(0, 2, 1, 3)
    degree_rows = degree.reshape(-1, LANES)
    gain = norm_gain[None, :]

    picked, mask, mask_t, recv = lax.optimization_barrier((select(send, node_feats), *unpack(count, words), recv))
    arrived = exchange(picked)
    products, feats, act, gate = edges_forward(recv, arrived, mask_t, mask, degree_rows, weight_in, weight_out)
    mine = gather_sum(send, exchange(products), nodes, width)
    updated, gain_part, picked = norm_and_select(send, mine, swap(mine), node_feats, cotangent, gain)
    arrived = exchange(picked)
    products = edges_backward(recv, arrived, mask_t, mask, degree_rows, weight_in, weight_out, feats, act, gate)
    arrived = exchange(products)

    weight_sums = tail_sum(arrived, width // LANES * TILE)
    extra = weight_sums.shape[0]
    chunk = jnp.concatenate([weight_sums, gain_part], 0)
    mine = gather_sum(send, arrived, nodes, width)
    both, chunk = lax.optimization_barrier((mine + swap(mine), chunk))
    everyone = lax.all_to_all(
        jnp.broadcast_to(chunk[None], (owners,) + chunk.shape), "wide", split_axis=0, concat_axis=0, tiled=True
    )
    grad_nodes = cotangent.astype(F32) + both

    grad_gain = everyone[:, extra : extra + width // LANES].sum(0).reshape(width)
    held = everyone[:, :extra]
    theirs = swap(held)
    grads = jnp.stack([jnp.where(core == 0, held, theirs), jnp.where(core == 0, theirs, held)], 1)
    grads = grads.reshape(-1, LANES)
    grad_out = jnp.concatenate(jnp.split(grads[: inner * width // LANES], width // LANES), 1)
    grad_in = jnp.concatenate(jnp.split(grads[inner * width // LANES :], inner // LANES), 1)

    edge_factor = (degree.shape[0] * owners * lax.axis_size("narrow")) ** (-0.5)
    return (
        updated,
        grad_nodes,
        grad_in * edge_factor,
        grad_out * edge_factor,
        grad_gain * (nodes * owners) ** (-0.5),
    )


def solution(mesh):
    return jax.shard_map(
        shards,
        mesh=mesh,
        in_specs=(
            P("wide", None),
            P("wide", None, "narrow", None),
            P("wide", "narrow", None, None),
            P("wide", "narrow", None),
            P("wide", "narrow", None, None, None, None),
            P(("wide", "narrow")),
            P(),
            P(),
            P(),
            P("wide", None),
        ),
        out_specs=(P("wide", None), P("wide", None), P(), P(), P()),
        check_vma=False,
    )
```

```python
import functools

import jax
import jax.numpy as jnp
from jax import lax
from jax.experimental import pallas as pl
from jax.experimental.pallas import tpu as pltpu
from jax.sharding import PartitionSpec as P

F32 = jnp.float32
BF16 = jnp.bfloat16
TILE = 128
LANES = 128
STEP_TILES = 8
EDGE_TILES = 64
EDGE_CHUNK = 1024
PARAMS = pltpu.CompilerParams(vmem_limit_bytes=14 * 1024 * 1024)


SMEM = pl.BlockSpec(memory_space=pltpu.SMEM)
VMEM = pl.BlockSpec(memory_space=pltpu.VMEM)


def dot(a, b, dims=((1,), (0,))):
    return lax.dot_general(a, b, (dims, ((), ())), preferred_element_type=F32)


def rows_at(block):
    return pl.ds(pl.multiple_of(block * TILE, TILE), TILE)


def unpack_kernel(count_ref, words_ref, mask_ref, mask_t_ref, done_ref):
    done_ref[...] = jnp.zeros_like(done_ref)
    step = pl.program_id(0)
    owners, words, slots, _ = words_ref.shape
    row = lax.broadcasted_iota(jnp.int32, (8, TILE), 0)
    for owner in range(owners):
        count = count_ref[step * owners + owner]
        for slot in range(slots):
            live = jnp.where(count > slot, jnp.int32(-1), jnp.int32(0))
            word = [jnp.broadcast_to(words_ref[owner, j, slot : slot + 1], (8, TILE)) & live for j in range(words)]
            groups = []
            for first in range(0, TILE, 8):
                low, high = first // 15, (first + 7) // 15
                picked = word[low]
                shift = row + (first - low * 15)
                if high != low:
                    later = row >= high * 15 - first
                    picked = jnp.where(later, word[high], picked)
                    shift = jnp.where(later, shift - 15, shift)
                groups.append((jnp.right_shift(picked, shift) & 1).astype(F32))
            mask = jnp.concatenate(groups, axis=0)
            mask_ref[owner * slots + slot] = mask.astype(BF16)
            mask_t_ref[owner * slots + slot] = mask.T.astype(BF16)


def unpack(count, words):
    owners, _, slots, _ = words.shape
    per = 8
    out = jax.ShapeDtypeStruct((owners * slots, TILE, TILE), BF16)
    block = pl.BlockSpec((per * slots, TILE, TILE), lambda i, c: (i, 0, 0))
    return pl.pallas_call(
        unpack_kernel,
        out_shape=(out, out, jax.ShapeDtypeStruct((8, LANES), F32)),
        grid_spec=pltpu.PrefetchScalarGridSpec(
            num_scalar_prefetch=1,
            grid=(owners // per,),
            in_specs=[pl.BlockSpec((per,) + words.shape[1:], lambda i, c: (i, 0, 0, 0))],
            out_specs=(block, block, pl.BlockSpec((8, LANES), lambda i, c: (0, 0))),
        ),
        compiler_params=PARAMS,
        name="unpack_masks",
    )(count, words)


def steps_of(tiles, size=STEP_TILES):
    return tiles.shape[0] // size


def select_kernel(send_ref, rows_ref, _, out_ref):
    def body(i, carry):
        for tile in range(STEP_TILES):
            out_ref[i * STEP_TILES + tile] = rows_ref[rows_at(send_ref[i * STEP_TILES + tile])]
        return carry

    lax.fori_loop(0, steps_of(out_ref), body, 0)


def select(send, rows, after):
    return pl.pallas_call(
        select_kernel,
        out_shape=jax.ShapeDtypeStruct((send.shape[0], TILE, rows.shape[1]), BF16),
        in_specs=[SMEM, VMEM, VMEM],
        out_specs=VMEM,
        compiler_params=PARAMS,
        name="select_blocks",
    )(send, rows, after)


def collect(recv_ref, arrived, mask_t, acc):
    acc[...] = jnp.zeros_like(acc)

    def body(i, carry):
        for tile in range(EDGE_TILES):
            where = rows_at(recv_ref[i * EDGE_TILES + tile])
            acc[where] += dot(mask_t[i * EDGE_TILES + tile], arrived[i * EDGE_TILES + tile])
        return carry

    lax.fori_loop(0, steps_of(arrived, EDGE_TILES), body, 0)


def spread(recv_ref, mask, values, made, grads=None):
    def body(i, carry):
        for tile in range(EDGE_TILES):
            where = rows_at(recv_ref[i * EDGE_TILES + tile])
            product = dot(mask[i * EDGE_TILES + tile], values[where]).astype(BF16)
            for h in range(product.shape[1] // LANES):
                made[i * EDGE_TILES + tile, h * TILE : (h + 1) * TILE] = product[:, h * LANES : (h + 1) * LANES]
            if grads is not None:
                first = product.shape[1] // LANES * TILE
                extra = made.shape[1] - first
                at = pl.ds(pl.multiple_of((i * EDGE_TILES + tile) * extra, extra), extra)
                made[i * EDGE_TILES + tile, first:] = grads[at].astype(BF16)
        return carry

    lax.fori_loop(0, steps_of(made, EDGE_TILES), body, 0)


def scaled(rows, degree_ref, i):
    blocks = rows.shape[0] // TILE
    parts = []
    for k in range(blocks):
        scale = lax.rsqrt(degree_ref[pl.ds(i * blocks + k, 1)].astype(F32))
        scale = jnp.broadcast_to(scale, (TILE, LANES)).T
        lanes = [rows[k * TILE : (k + 1) * TILE, j : j + LANES] * scale for j in range(0, rows.shape[1], LANES)]
        parts.append(jnp.concatenate(lanes, axis=1))
    return jnp.concatenate(parts, axis=0)


def forward_kernel(
    recv_ref, arrived, mask_t, mask, degree_ref, w_in_ref, w_out_ref, made, feats, act, gate, acc, values
):
    collect(recv_ref, arrived, mask_t, acc)
    chunk = min(EDGE_CHUNK, acc.shape[0])

    def body(i, carry):
        at = pl.ds(pl.multiple_of(i * chunk, chunk), chunk)
        rows = scaled(acc[at], degree_ref, i).astype(BF16)
        feats[at] = rows
        pre = dot(rows, w_in_ref[...])
        sig = jax.nn.sigmoid(pre)
        hidden = (pre * sig).astype(BF16)
        act[at] = hidden
        gate[at] = sig * (1.0 + pre * (1.0 - sig))
        values[at] = dot(hidden, w_out_ref[...]).astype(BF16)
        return carry

    lax.fori_loop(0, acc.shape[0] // chunk, body, 0)
    spread(recv_ref, mask, values, made)


def backward_kernel(
    recv_ref, arrived, mask_t, mask, degree_ref, w_in_ref, w_out_ref, feats, act, gate, made, acc, values, grads
):
    grads[...] = jnp.zeros_like(grads)
    collect(recv_ref, arrived, mask_t, acc)
    chunk = min(EDGE_CHUNK, acc.shape[0])

    def body(i, carry):
        at = pl.ds(pl.multiple_of(i * chunk, chunk), chunk)
        d_edge = acc[at].astype(BF16)
        d_act = dot(d_edge, w_out_ref[...], ((1,), (1,)))
        d_pre = (d_act * gate[at]).astype(BF16)
        values[at] = scaled(dot(d_pre, w_in_ref[...], ((1,), (1,))), degree_ref, i).astype(BF16)
        first = 0
        for grad in (dot(act[at], d_edge, ((0,), (0,))), dot(feats[at], d_pre, ((0,), (0,)))):
            for lane in range(0, grad.shape[1], LANES):
                grads[first : first + grad.shape[0]] += grad[:, lane : lane + LANES]
                first += grad.shape[0]
        return carry

    lax.fori_loop(0, acc.shape[0] // chunk, body, 0)
    spread(recv_ref, mask, values, made, grads)


def edges_forward(recv, arrived, mask_t, mask, degree, w_in, w_out):
    tiles = arrived.shape[0]
    edges, width, inner = degree.size, w_in.shape[0], w_in.shape[1]
    rows = width // LANES * TILE
    return pl.pallas_call(
        forward_kernel,
        out_shape=(
            jax.ShapeDtypeStruct((tiles, rows, LANES), BF16),
            jax.ShapeDtypeStruct((edges, width), BF16),
            jax.ShapeDtypeStruct((edges, inner), BF16),
            jax.ShapeDtypeStruct((edges, inner), F32),
        ),
        in_specs=[SMEM] + [VMEM] * 6,
        out_specs=(VMEM,) * 4,
        scratch_shapes=[
            pltpu.VMEM((edges, width), F32),
            pltpu.VMEM((edges, width), BF16),
        ],
        compiler_params=PARAMS,
        name="edges_forward",
    )(recv, arrived, mask_t, mask, degree, w_in, w_out)


def edges_backward(recv, arrived, mask_t, mask, degree, w_in, w_out, feats, act, gate):
    tiles = arrived.shape[0]
    edges, width, inner = degree.size, w_in.shape[0], w_in.shape[1]
    grad_rows = 2 * inner * width // LANES
    rows = width // LANES * TILE + grad_rows // tiles
    return pl.pallas_call(
        backward_kernel,
        out_shape=jax.ShapeDtypeStruct((tiles, rows, LANES), BF16),
        in_specs=[SMEM] + [VMEM] * 9,
        out_specs=VMEM,
        scratch_shapes=[
            pltpu.VMEM((edges, width), F32),
            pltpu.VMEM((edges, width), BF16),
            pltpu.VMEM((grad_rows, LANES), F32),
        ],
        compiler_params=PARAMS,
        name="edges_backward",
    )(recv, arrived, mask_t, mask, degree, w_in, w_out, feats, act, gate)


def gather_sum_kernel(send_ref, arrived, out_ref):
    out_ref[...] = jnp.zeros_like(out_ref)

    def body(i, carry):
        for tile in range(STEP_TILES):
            where = rows_at(send_ref[i * STEP_TILES + tile])
            for h in range(out_ref.shape[1] // LANES):
                rows = arrived[i * STEP_TILES + tile, h * TILE : (h + 1) * TILE]
                out_ref[where, h * LANES : (h + 1) * LANES] += rows.astype(F32)
        return carry

    lax.fori_loop(0, steps_of(arrived), body, 0)


def gather_sum(send, arrived, nodes, width):
    return pl.pallas_call(
        gather_sum_kernel,
        out_shape=jax.ShapeDtypeStruct((nodes, width), F32),
        in_specs=[SMEM, VMEM],
        out_specs=VMEM,
        compiler_params=PARAMS,
        name="node_sums",
    )(send, arrived)


def tail_sum_kernel(arrived_ref, out_ref):
    rows = out_ref.shape[0]
    out_ref[...] = jnp.sum(arrived_ref[:, arrived_ref.shape[1] - rows :].astype(F32), axis=0)


def tail_sum(arrived, rows):
    return pl.pallas_call(
        tail_sum_kernel,
        out_shape=jax.ShapeDtypeStruct((arrived.shape[1] - rows, arrived.shape[2]), F32),
        in_specs=[VMEM],
        out_specs=VMEM,
        compiler_params=PARAMS,
        name="weight_sums",
    )(arrived)


def norm_kernel(
    send_ref, mine_ref, other_ref, feats_ref, cot_ref, gain_ref, updated_ref, part_ref, out_ref, d_summed
):
    gain = gain_ref[...]

    def body(i, part):
        at = rows_at(i)
        summed = mine_ref[at] + other_ref[at]
        inv_rms = lax.rsqrt(jnp.mean(summed * summed, axis=-1, keepdims=True) + 1e-05)
        normed = summed * inv_rms
        updated_ref[at] = (feats_ref[at].astype(F32) + normed * gain).astype(BF16)
        upstream = cot_ref[at].astype(F32)
        d_normed = upstream * gain
        inner = jnp.mean(d_normed * normed, axis=-1, keepdims=True)
        d_summed[at] = (inv_rms * (d_normed - normed * inner)).astype(BF16)
        return part + jnp.sum((upstream * normed).reshape(TILE // 8, 8, -1), axis=0)

    parts = lax.fori_loop(0, mine_ref.shape[0] // TILE, body, jnp.zeros((8, mine_ref.shape[1]), F32))
    row = jnp.sum(parts, axis=0, keepdims=True)
    high = row.astype(BF16).astype(F32)
    rows = [part[:, i : i + LANES] for part in (high, row - high) for i in range(0, row.shape[1], LANES)]
    rows.append(jnp.zeros((part_ref.shape[0] - len(rows), LANES), F32))
    part_ref[...] = jnp.concatenate(rows, axis=0).astype(BF16)

    select_kernel(send_ref, d_summed, None, out_ref)


def norm_and_select(send, mine, other, feats, cot, gain):
    nodes, width = feats.shape
    updated, gain_part, out = pl.pallas_call(
        norm_kernel,
        out_shape=(
            jax.ShapeDtypeStruct((nodes, width), BF16),
            jax.ShapeDtypeStruct((16, LANES), BF16),
            jax.ShapeDtypeStruct((send.shape[0], TILE, width), BF16),
        ),
        in_specs=[SMEM] + [VMEM] * 5,
        out_specs=(VMEM,) * 3,
        scratch_shapes=[pltpu.VMEM((nodes, width), BF16)],
        compiler_params=PARAMS,
        name="norm_and_select",
    )(send, mine, other, feats, cot, gain)
    return updated, gain_part, out


def exchange(tiles):
    return lax.all_to_all(tiles, ("wide", "narrow"), split_axis=0, concat_axis=0, tiled=True)


def swap(rows):
    return lax.ppermute(rows, "narrow", [(0, 1), (1, 0)])


def shards(
    node_feats,
    send_block,
    recv_block,
    tile_count,
    mask_bits,
    degree,
    weight_in,
    weight_out,
    norm_gain,
    cotangent,
):
    owners = lax.axis_size("wide")
    nodes, width = node_feats.shape
    inner = weight_in.shape[1]
    core = lax.axis_index("narrow")
    my_slots = send_block[0, :, 0, :]
    own = lax.dynamic_index_in_dim(my_slots, core, 1, keepdims=False)
    theirs = swap(lax.dynamic_index_in_dim(my_slots, 1 - core, 1, keepdims=False))
    send = jnp.where(core == 0, jnp.stack([own, theirs], 1), jnp.stack([theirs, own], 1)).reshape(-1)
    recv = recv_block.reshape(-1)
    count = tile_count.reshape(-1)
    words = mask_bits[0, 0].transpose(0, 2, 1, 3)
    degree_rows = degree.reshape(-1, LANES)
    gain = norm_gain[None, :]

    mask, mask_t, unpacked = unpack(count, words)
    picked, recv = lax.optimization_barrier((select(send, node_feats, unpacked), recv))
    arrived = exchange(picked)
    products, feats, act, gate = edges_forward(recv, arrived, mask_t, mask, degree_rows, weight_in, weight_out)
    mine = gather_sum(send, exchange(products), nodes, width)
    updated, gain_part, picked = norm_and_select(send, mine, swap(mine), node_feats, cotangent, gain)
    arrived = exchange(picked)
    products = edges_backward(recv, arrived, mask_t, mask, degree_rows, weight_in, weight_out, feats, act, gate)
    arrived = exchange(products)

    weight_sums = tail_sum(arrived, width // LANES * TILE)
    extra = weight_sums.shape[0]
    gain_rows = width // LANES
    chunk = jnp.concatenate([weight_sums.astype(BF16), gain_part[: max(8, 2 * gain_rows)]], 0)
    mine = gather_sum(send, arrived, nodes, width)
    grad_nodes = cotangent.astype(F32) + (mine + swap(mine))
    grad_nodes, chunk = lax.optimization_barrier((grad_nodes, chunk))
    everyone = lax.all_to_all(
        jnp.broadcast_to(chunk[None], (owners,) + chunk.shape), "wide", split_axis=0, concat_axis=0, tiled=True
    )

    gains = everyone[:, extra : extra + 2 * gain_rows].astype(F32).sum(0)
    grad_gain = (gains[:gain_rows] + gains[gain_rows:]).reshape(width)
    held = everyone[:, :extra]
    theirs = swap(held)
    grads = jnp.stack([jnp.where(core == 0, held, theirs), jnp.where(core == 0, theirs, held)], 1)
    grads = grads.reshape(-1, LANES).astype(F32)
    grad_out = jnp.concatenate(jnp.split(grads[: inner * width // LANES], width // LANES), 1)
    grad_in = jnp.concatenate(jnp.split(grads[inner * width // LANES :], inner // LANES), 1)

    edge_factor = (degree.shape[0] * owners * lax.axis_size("narrow")) ** (-0.5)
    return (
        updated,
        grad_nodes,
        grad_in * edge_factor,
        grad_out * edge_factor,
        grad_gain * (nodes * owners) ** (-0.5),
    )


def solution(mesh):
    return jax.shard_map(
        shards,
        mesh=mesh,
        in_specs=(
            P("wide", None),
            P("wide", None, "narrow", None),
            P("wide", "narrow", None, None),
            P("wide", "narrow", None),
            P("wide", "narrow", None, None, None, None),
            P(("wide", "narrow")),
            P(),
            P(),
            P(),
            P("wide", None),
        ),
        out_specs=(P("wide", None), P("wide", None), P(), P(), P()),
        check_vma=False,
    )
```

```python
import functools

import jax
import jax.numpy as jnp
from jax import lax
from jax.experimental import pallas as pl
from jax.experimental.pallas import tpu as pltpu
from jax.sharding import PartitionSpec as P

F32 = jnp.float32
BF16 = jnp.bfloat16
TILE = 128
HALF = TILE // 2
LANES = 128
STEP_TILES = 8
EDGE_TILES = 64
EDGE_CHUNK = 1024
PARAMS = pltpu.CompilerParams(vmem_limit_bytes=14 * 1024 * 1024)


SMEM = pl.BlockSpec(memory_space=pltpu.SMEM)
VMEM = pl.BlockSpec(memory_space=pltpu.VMEM)


def dot(a, b, dims=((1,), (0,))):
    return lax.dot_general(a, b, (dims, ((), ())), preferred_element_type=F32)


def rows_at(block):
    return pl.ds(pl.multiple_of(block * TILE, TILE), TILE)


def unpack_tile(word, row):
    groups = []
    for first in range(0, TILE, 8):
        low, high = first // 15, (first + 7) // 15
        picked = word[low]
        shift = row + (first - low * 15)
        if high != low:
            later = row >= high * 15 - first
            picked = jnp.where(later, word[high], picked)
            shift = jnp.where(later, shift - 15, shift)
        groups.append((jnp.right_shift(picked, shift) & 1).astype(F32))
    return jnp.concatenate(groups, axis=0)


def unpack(count_ref, words_ref, mask_ref, mask_t_ref):
    owners, words, slots, _ = words_ref.shape
    per = 8

    def body(i, carry):
        row = lax.broadcasted_iota(jnp.int32, (8, TILE), 0)
        for k in range(per):
            owner = i * per + k
            count = count_ref[owner]
            for slot in range(slots):
                live = jnp.where(count > slot, jnp.int32(-1), jnp.int32(0))
                word = [
                    jnp.broadcast_to(words_ref[owner, j, slot : slot + 1], (8, TILE)) & live for j in range(words)
                ]
                mask = unpack_tile(word, row)
                mask_ref[owner * slots + slot] = mask.astype(BF16)
                mask_t_ref[owner * slots + slot] = mask.T.astype(BF16)
        return carry

    lax.fori_loop(0, owners // per, body, 0)


def steps_of(tiles, size=STEP_TILES):
    return tiles.shape[0] // size


def half_at(block):
    return pl.ds(pl.multiple_of(block * HALF, HALF), HALF)


def select_kernel(send_ref, rows_ref, out_ref):
    slots = out_ref.shape[1] // HALF

    def body(i, carry):
        for tile in range(STEP_TILES):
            for k in range(slots):
                block = send_ref[(i * STEP_TILES + tile) * slots + k]
                out_ref[i * STEP_TILES + tile, k * HALF : (k + 1) * HALF] = rows_ref[half_at(block)]
        return carry

    lax.fori_loop(0, steps_of(out_ref), body, 0)


def select(send, rows, devices):
    return pl.pallas_call(
        select_kernel,
        out_shape=jax.ShapeDtypeStruct((devices, send.shape[0] // devices * HALF, rows.shape[1]), BF16),
        in_specs=[SMEM, VMEM],
        out_specs=VMEM,
        compiler_params=PARAMS,
        name="select_blocks",
    )(send, rows)


def collect(recv_ref, arrived, mask_t, acc):
    acc[...] = jnp.zeros_like(acc)

    def body(i, carry):
        for k in range(EDGE_TILES):
            tile = i * EDGE_TILES + k
            owner, slot = i * (EDGE_TILES // 2) + k // 2, k % 2
            halves = [arrived[2 * owner + c, slot * HALF : (slot + 1) * HALF] for c in range(2)]
            acc[rows_at(recv_ref[tile])] += dot(mask_t[tile], jnp.concatenate(halves, axis=0))
        return carry

    lax.fori_loop(0, steps_of(arrived, EDGE_TILES), body, 0)


def spread(recv_ref, mask, values, made, grads=None):
    pieces = values.shape[1] // LANES
    first = 2 * pieces * HALF

    def body(i, carry):
        for k in range(EDGE_TILES):
            tile = i * EDGE_TILES + k
            owner, slot = i * (EDGE_TILES // 2) + k // 2, k % 2
            product = dot(mask[tile], values[rows_at(recv_ref[tile])]).astype(BF16)
            for c in range(2):
                for h in range(pieces):
                    at = (slot * pieces + h) * HALF
                    made[2 * owner + c, at : at + HALF] = product[
                        c * HALF : (c + 1) * HALF, h * LANES : (h + 1) * LANES
                    ]
            if grads is not None:
                extra = made.shape[1] - first
                made[tile, first:] = grads[pl.ds(pl.multiple_of(tile * extra, extra), extra)].astype(BF16)
        return carry

    lax.fori_loop(0, steps_of(made, EDGE_TILES), body, 0)


def scaled(rows, degree_ref, i):
    blocks = rows.shape[0] // TILE
    parts = []
    for k in range(blocks):
        scale = lax.rsqrt(degree_ref[pl.ds(i * blocks + k, 1)].astype(F32))
        scale = jnp.broadcast_to(scale, (TILE, LANES)).T
        lanes = [rows[k * TILE : (k + 1) * TILE, j : j + LANES] * scale for j in range(0, rows.shape[1], LANES)]
        parts.append(jnp.concatenate(lanes, axis=1))
    return jnp.concatenate(parts, axis=0)


def forward_kernel(
    recv_ref, count_ref, arrived, words_ref, degree_ref, w_in_ref, w_out_ref,
    made, mask_t, mask, feats, act, gate, acc, values,
):
    unpack(count_ref, words_ref, mask, mask_t)
    collect(recv_ref, arrived, mask_t, acc)
    chunk = min(EDGE_CHUNK, acc.shape[0])

    def body(i, carry):
        at = pl.ds(pl.multiple_of(i * chunk, chunk), chunk)
        rows = scaled(acc[at], degree_ref, i).astype(BF16)
        feats[at] = rows
        pre = dot(rows, w_in_ref[...])
        sig = jax.nn.sigmoid(pre)
        hidden = (pre * sig).astype(BF16)
        act[at] = hidden
        gate[at] = sig * (1.0 + pre * (1.0 - sig))
        values[at] = dot(hidden, w_out_ref[...]).astype(BF16)
        return carry

    lax.fori_loop(0, acc.shape[0] // chunk, body, 0)
    spread(recv_ref, mask, values, made)


def backward_kernel(
    recv_ref, arrived, mask_t, mask, degree_ref, w_in_ref, w_out_ref, feats, act, gate, made, acc, values, grads
):
    grads[...] = jnp.zeros_like(grads)
    collect(recv_ref, arrived, mask_t, acc)
    chunk = min(EDGE_CHUNK, acc.shape[0])

    def body(i, carry):
        at = pl.ds(pl.multiple_of(i * chunk, chunk), chunk)
        d_edge = acc[at].astype(BF16)
        d_act = dot(d_edge, w_out_ref[...], ((1,), (1,)))
        d_pre = (d_act * gate[at]).astype(BF16)
        values[at] = scaled(dot(d_pre, w_in_ref[...], ((1,), (1,))), degree_ref, i).astype(BF16)
        first = 0
        for grad in (dot(act[at], d_edge, ((0,), (0,))), dot(feats[at], d_pre, ((0,), (0,)))):
            for lane in range(0, grad.shape[1], LANES):
                grads[first : first + grad.shape[0]] += grad[:, lane : lane + LANES]
                first += grad.shape[0]
        return carry

    lax.fori_loop(0, acc.shape[0] // chunk, body, 0)
    spread(recv_ref, mask, values, made, grads)


def edges_forward(recv, count, arrived, words, degree, w_in, w_out):
    tiles = arrived.shape[0]
    edges, width, inner = degree.size, w_in.shape[0], w_in.shape[1]
    rows = width // LANES * TILE
    return pl.pallas_call(
        forward_kernel,
        out_shape=(
            jax.ShapeDtypeStruct((tiles, rows, LANES), BF16),
            jax.ShapeDtypeStruct((tiles, TILE, TILE), BF16),
            jax.ShapeDtypeStruct((tiles, TILE, TILE), BF16),
            jax.ShapeDtypeStruct((edges, width), BF16),
            jax.ShapeDtypeStruct((edges, inner), BF16),
            jax.ShapeDtypeStruct((edges, inner), F32),
        ),
        in_specs=[SMEM] * 2 + [VMEM] * 5,
        out_specs=(VMEM,) * 6,
        scratch_shapes=[
            pltpu.VMEM((edges, width), F32),
            pltpu.VMEM((edges, width), BF16),
        ],
        compiler_params=PARAMS,
        name="edges_forward",
    )(recv, count, arrived, words, degree, w_in, w_out)


def edges_backward(recv, arrived, mask_t, mask, degree, w_in, w_out, feats, act, gate):
    tiles = arrived.shape[0]
    edges, width, inner = degree.size, w_in.shape[0], w_in.shape[1]
    grad_rows = 2 * inner * width // LANES
    rows = width // LANES * TILE + grad_rows // tiles
    return pl.pallas_call(
        backward_kernel,
        out_shape=jax.ShapeDtypeStruct((tiles, rows, LANES), BF16),
        in_specs=[SMEM] + [VMEM] * 9,
        out_specs=VMEM,
        scratch_shapes=[
            pltpu.VMEM((edges, width), F32),
            pltpu.VMEM((edges, width), BF16),
            pltpu.VMEM((grad_rows, LANES), F32),
        ],
        compiler_params=PARAMS,
        name="edges_backward",
    )(recv, arrived, mask_t, mask, degree, w_in, w_out, feats, act, gate)


def sum_products(send_ref, arrived, acc):
    pieces = acc.shape[1] // LANES
    acc[...] = jnp.zeros_like(acc)

    def body(i, carry):
        for k in range(2 * STEP_TILES):
            source, slot = i * STEP_TILES + k // 2, k % 2
            where = half_at(send_ref[2 * source + slot])
            for h in range(pieces):
                at = (slot * pieces + h) * HALF
                acc[where, h * LANES : (h + 1) * LANES] += arrived[source, at : at + HALF].astype(F32)
        return carry

    lax.fori_loop(0, steps_of(arrived), body, 0)


def grad_kernel(send_ref, arrived, cot_ref, out_ref, acc):
    sum_products(send_ref, arrived, acc)
    out_ref[...] = cot_ref[...].astype(F32) + acc[...]


def node_grads(send, arrived, cot):
    return pl.pallas_call(
        grad_kernel,
        out_shape=jax.ShapeDtypeStruct(cot.shape, F32),
        in_specs=[SMEM, VMEM, VMEM],
        out_specs=VMEM,
        scratch_shapes=[pltpu.VMEM(cot.shape, F32)],
        compiler_params=PARAMS,
        name="node_grads",
    )(send, arrived, cot)


def tail_sum_kernel(arrived_ref, out_ref):
    rows = out_ref.shape[0]
    out_ref[...] = jnp.sum(arrived_ref[:, arrived_ref.shape[1] - rows :].astype(F32), axis=0)


def tail_sum(arrived, rows):
    return pl.pallas_call(
        tail_sum_kernel,
        out_shape=jax.ShapeDtypeStruct((arrived.shape[1] - rows, arrived.shape[2]), F32),
        in_specs=[VMEM],
        out_specs=VMEM,
        compiler_params=PARAMS,
        name="weight_sums",
    )(arrived)


def norm_kernel(
    send_ref, arrived, feats_ref, cot_ref, gain_ref, updated_ref, part_ref, out_ref, acc, d_summed
):
    sum_products(send_ref, arrived, acc)
    gain = gain_ref[...]

    def body(i, part):
        at = rows_at(i)
        summed = acc[at]
        inv_rms = lax.rsqrt(jnp.mean(summed * summed, axis=-1, keepdims=True) + 1e-05)
        normed = summed * inv_rms
        updated_ref[at] = (feats_ref[at].astype(F32) + normed * gain).astype(BF16)
        upstream = cot_ref[at].astype(F32)
        d_normed = upstream * gain
        inner = jnp.mean(d_normed * normed, axis=-1, keepdims=True)
        d_summed[at] = (inv_rms * (d_normed - normed * inner)).astype(BF16)
        return part + jnp.sum((upstream * normed).reshape(TILE // 8, 8, -1), axis=0)

    parts = lax.fori_loop(0, acc.shape[0] // TILE, body, jnp.zeros((8, acc.shape[1]), F32))
    row = jnp.sum(parts, axis=0, keepdims=True)
    high = row.astype(BF16).astype(F32)
    rows = [part[:, i : i + LANES] for part in (high, row - high) for i in range(0, row.shape[1], LANES)]
    rows.append(jnp.zeros((part_ref.shape[0] - len(rows), LANES), F32))
    part_ref[...] = jnp.concatenate(rows, axis=0).astype(BF16)

    select_kernel(send_ref, d_summed, out_ref)


def norm_and_select(send, arrived, feats, cot, gain):
    nodes, width = feats.shape
    devices = arrived.shape[0]
    return pl.pallas_call(
        norm_kernel,
        out_shape=(
            jax.ShapeDtypeStruct((nodes, width), BF16),
            jax.ShapeDtypeStruct((16, LANES), BF16),
            jax.ShapeDtypeStruct((devices, send.shape[0] // devices * HALF, width), BF16),
        ),
        in_specs=[SMEM] + [VMEM] * 4,
        out_specs=(VMEM,) * 3,
        scratch_shapes=[pltpu.VMEM((nodes, width), F32), pltpu.VMEM((nodes, width), BF16)],
        compiler_params=PARAMS,
        name="norm_and_select",
    )(send, arrived, feats, cot, gain)


def exchange(tiles):
    return lax.all_to_all(tiles, ("wide", "narrow"), split_axis=0, concat_axis=0, tiled=True)


def swap(rows):
    return lax.ppermute(rows, "narrow", [(0, 1), (1, 0)])


def shards(
    node_feats,
    send_block,
    recv_block,
    tile_count,
    mask_bits,
    degree,
    weight_in,
    weight_out,
    norm_gain,
    cotangent,
):
    owners = lax.axis_size("wide")
    nodes, width = node_feats.shape
    inner = weight_in.shape[1]
    core = lax.axis_index("narrow")
    devices = 2 * owners
    by_core = lambda mine, theirs: (jnp.where(core == 0, mine, theirs), jnp.where(core == 0, theirs, mine))
    my_slots = send_block[0, :, 0, :]
    send = jnp.stack(by_core(my_slots, swap(my_slots)), 1).reshape(-1)
    recv = recv_block.reshape(-1)
    count = tile_count.reshape(-1)
    words = mask_bits[0, 0].transpose(0, 2, 1, 3)
    degree_rows = degree.reshape(-1, LANES)
    half_of = lambda rows: lax.dynamic_index_in_dim(
        rows.reshape(-1, 2, HALF, width), core, 1, keepdims=False
    ).reshape(-1, width)
    whole_of = lambda mine, theirs: jnp.stack(
        [half.reshape(-1, HALF, width) for half in by_core(mine, theirs)], 1
    ).reshape(nodes, width)

    feats_half, cot_half = half_of(node_feats), half_of(cotangent)
    picked, recv, count, words, cot_half = lax.optimization_barrier(
        (select(send, feats_half, devices), recv, count, words, cot_half)
    )
    arrived = exchange(picked)
    products, mask_t, mask, feats, act, gate = edges_forward(
        recv, count, arrived, words, degree_rows, weight_in, weight_out
    )
    updated, gain_part, picked = norm_and_select(send, exchange(products), feats_half, cot_half, norm_gain[None, :])
    arrived = exchange(picked)
    products = edges_backward(recv, arrived, mask_t, mask, degree_rows, weight_in, weight_out, feats, act, gate)
    arrived = exchange(products)

    arrived, updated, gain_part = lax.optimization_barrier((arrived, updated, gain_part))
    weight_sums = tail_sum(arrived, 2 * width // LANES * HALF)
    extra = weight_sums.shape[0]
    gain_rows = width // LANES
    chunk = jnp.concatenate([weight_sums.astype(BF16), gain_part[: max(8, 2 * gain_rows)]], 0)
    grads_half = node_grads(send, arrived, cot_half)
    grads_other, updated_other, chunk = lax.optimization_barrier((swap(grads_half), swap(updated), chunk))
    everyone = lax.all_to_all(
        jnp.broadcast_to(chunk[None], (owners,) + chunk.shape), "wide", split_axis=0, concat_axis=0, tiled=True
    )
    grad_nodes = whole_of(grads_half, grads_other)
    updated = whole_of(updated, updated_other)

    theirs = swap(everyone)
    gains = (everyone[:, extra : extra + 2 * gain_rows], theirs[:, extra : extra + 2 * gain_rows])
    gains = sum(g.astype(F32).sum(0) for g in by_core(*gains))
    grad_gain = (gains[:gain_rows] + gains[gain_rows:]).reshape(width)
    grads = jnp.stack(by_core(everyone[:, :extra], theirs[:, :extra]), 1)
    grads = grads.reshape(-1, LANES).astype(F32)
    grad_out = jnp.concatenate(jnp.split(grads[: inner * width // LANES], width // LANES), 1)
    grad_in = jnp.concatenate(jnp.split(grads[inner * width // LANES :], inner // LANES), 1)

    edge_factor = (degree.shape[0] * owners * lax.axis_size("narrow")) ** (-0.5)
    return (
        updated,
        grad_nodes,
        grad_in * edge_factor,
        grad_out * edge_factor,
        grad_gain * (nodes * owners) ** (-0.5),
    )


def solution(mesh):
    return jax.shard_map(
        shards,
        mesh=mesh,
        in_specs=(
            P("wide", None),
            P("wide", None, "narrow", None),
            P("wide", "narrow", None, None),
            P("wide", "narrow", None),
            P("wide", "narrow", None, None, None, None),
            P(("wide", "narrow")),
            P(),
            P(),
            P(),
            P("wide", None),
        ),
        out_specs=(P("wide", None), P("wide", None), P(), P(), P()),
        check_vma=False,
    )
```

```python
import functools

import jax
import jax.numpy as jnp
from jax import lax
from jax.experimental import pallas as pl
from jax.experimental.pallas import tpu as pltpu
from jax.sharding import PartitionSpec as P

F32 = jnp.float32
BF16 = jnp.bfloat16
TILE = 128
HALF = TILE // 2
LANES = 128
STEP_TILES = 8
EDGE_TILES = 64
EDGE_CHUNK = 1024
PARAMS = pltpu.CompilerParams(vmem_limit_bytes=14 * 1024 * 1024)


SMEM = pl.BlockSpec(memory_space=pltpu.SMEM)
VMEM = pl.BlockSpec(memory_space=pltpu.VMEM)


def dot(a, b, dims=((1,), (0,))):
    return lax.dot_general(a, b, (dims, ((), ())), preferred_element_type=F32)


def rows_at(block):
    return pl.ds(pl.multiple_of(block * TILE, TILE), TILE)


def unpack_tile(word, row):
    groups = []
    for first in range(0, TILE, 8):
        low, high = first // 15, (first + 7) // 15
        picked = word[low]
        shift = row + (first - low * 15)
        if high != low:
            later = row >= high * 15 - first
            picked = jnp.where(later, word[high], picked)
            shift = jnp.where(later, shift - 15, shift)
        groups.append((jnp.right_shift(picked, shift) & 1).astype(F32))
    return jnp.concatenate(groups, axis=0)


def unpack(count_ref, words_ref, owner, slot):
    live = jnp.where(count_ref[owner] > slot, jnp.int32(-1), jnp.int32(0))
    row = lax.broadcasted_iota(jnp.int32, (8, TILE), 0)
    return unpack_tile(
        [
            jnp.broadcast_to(words_ref[owner, j, slot : slot + 1], (8, TILE)) & live
            for j in range(words_ref.shape[1])
        ],
        row,
    )


def steps_of(tiles, size=STEP_TILES):
    return tiles.shape[0] // size


def half_at(block):
    return pl.ds(pl.multiple_of(block * HALF, HALF), HALF)


def select_kernel(send_ref, rows_ref, out_ref):
    slots = out_ref.shape[1] // HALF

    def body(i, carry):
        for tile in range(STEP_TILES):
            for k in range(slots):
                block = send_ref[(i * STEP_TILES + tile) * slots + k]
                out_ref[i * STEP_TILES + tile, k * HALF : (k + 1) * HALF] = rows_ref[half_at(block)]
        return carry

    lax.fori_loop(0, steps_of(out_ref), body, 0)


def select(send, rows, devices):
    return pl.pallas_call(
        select_kernel,
        out_shape=jax.ShapeDtypeStruct((devices, send.shape[0] // devices * HALF, rows.shape[1]), BF16),
        in_specs=[SMEM, VMEM],
        out_specs=VMEM,
        compiler_params=PARAMS,
        name="select_blocks",
    )(send, rows)


def collect(recv_ref, arrived, mask_t, acc, unpacked=None):
    acc[...] = jnp.zeros_like(acc)

    def body(i, carry):
        for k in range(EDGE_TILES):
            tile = i * EDGE_TILES + k
            owner, slot = i * (EDGE_TILES // 2) + k // 2, k % 2
            halves = [arrived[2 * owner + c, slot * HALF : (slot + 1) * HALF] for c in range(2)]
            if unpacked is not None:
                count_ref, words_ref, mask = unpacked
                bits = unpack(count_ref, words_ref, owner, slot)
                mask[tile] = bits.astype(BF16)
                mask_t[tile] = bits.T.astype(BF16)
            acc[rows_at(recv_ref[tile])] += dot(mask_t[tile], jnp.concatenate(halves, axis=0))
        return carry

    lax.fori_loop(0, steps_of(arrived, EDGE_TILES), body, 0)


def spread(recv_ref, mask, values, made, grads=None):
    pieces = values.shape[1] // LANES
    first = 2 * pieces * HALF

    def body(i, carry):
        for k in range(EDGE_TILES):
            tile = i * EDGE_TILES + k
            owner, slot = i * (EDGE_TILES // 2) + k // 2, k % 2
            product = dot(mask[tile], values[rows_at(recv_ref[tile])]).astype(BF16)
            for c in range(2):
                for h in range(pieces):
                    at = (slot * pieces + h) * HALF
                    made[2 * owner + c, at : at + HALF] = product[
                        c * HALF : (c + 1) * HALF, h * LANES : (h + 1) * LANES
                    ]
            if grads is not None:
                extra = made.shape[1] - first
                made[tile, first:] = grads[pl.ds(pl.multiple_of(tile * extra, extra), extra)].astype(BF16)
        return carry

    lax.fori_loop(0, steps_of(made, EDGE_TILES), body, 0)


def scaled(rows, degree_ref, i):
    blocks = rows.shape[0] // TILE
    parts = []
    for k in range(blocks):
        scale = lax.rsqrt(degree_ref[pl.ds(i * blocks + k, 1)].astype(F32))
        scale = jnp.broadcast_to(scale, (TILE, LANES)).T
        lanes = [rows[k * TILE : (k + 1) * TILE, j : j + LANES] * scale for j in range(0, rows.shape[1], LANES)]
        parts.append(jnp.concatenate(lanes, axis=1))
    return jnp.concatenate(parts, axis=0)


def forward_kernel(
    recv_ref, count_ref, arrived, words_ref, degree_ref, w_in_ref, w_out_ref,
    made, mask_t, mask, feats, act, gate, acc, values,
):
    collect(recv_ref, arrived, mask_t, acc, (count_ref, words_ref, mask))
    chunk = min(EDGE_CHUNK, acc.shape[0])

    def body(i, carry):
        at = pl.ds(pl.multiple_of(i * chunk, chunk), chunk)
        rows = scaled(acc[at], degree_ref, i).astype(BF16)
        feats[at] = rows
        pre = dot(rows, w_in_ref[...])
        sig = jax.nn.sigmoid(pre)
        hidden = (pre * sig).astype(BF16)
        act[at] = hidden
        gate[at] = sig * (1.0 + pre * (1.0 - sig))
        values[at] = dot(hidden, w_out_ref[...]).astype(BF16)
        return carry

    lax.fori_loop(0, acc.shape[0] // chunk, body, 0)
    spread(recv_ref, mask, values, made)


def backward_kernel(
    recv_ref, arrived, mask_t, mask, degree_ref, w_in_ref, w_out_ref, feats, act, gate, made, acc, values, grads
):
    grads[...] = jnp.zeros_like(grads)
    collect(recv_ref, arrived, mask_t, acc)
    chunk = min(EDGE_CHUNK, acc.shape[0])

    def body(i, carry):
        at = pl.ds(pl.multiple_of(i * chunk, chunk), chunk)
        d_edge = acc[at].astype(BF16)
        d_act = dot(d_edge, w_out_ref[...], ((1,), (1,)))
        d_pre = (d_act * gate[at]).astype(BF16)
        values[at] = scaled(dot(d_pre, w_in_ref[...], ((1,), (1,))), degree_ref, i).astype(BF16)
        first = 0
        for grad in (dot(act[at], d_edge, ((0,), (0,))), dot(feats[at], d_pre, ((0,), (0,)))):
            for lane in range(0, grad.shape[1], LANES):
                grads[first : first + grad.shape[0]] += grad[:, lane : lane + LANES]
                first += grad.shape[0]
        return carry

    lax.fori_loop(0, acc.shape[0] // chunk, body, 0)
    spread(recv_ref, mask, values, made, grads)


def edges_forward(recv, count, arrived, words, degree, w_in, w_out):
    tiles = arrived.shape[0]
    edges, width, inner = degree.size, w_in.shape[0], w_in.shape[1]
    rows = width // LANES * TILE
    return pl.pallas_call(
        forward_kernel,
        out_shape=(
            jax.ShapeDtypeStruct((tiles, rows, LANES), BF16),
            jax.ShapeDtypeStruct((tiles, TILE, TILE), BF16),
            jax.ShapeDtypeStruct((tiles, TILE, TILE), BF16),
            jax.ShapeDtypeStruct((edges, width), BF16),
            jax.ShapeDtypeStruct((edges, inner), BF16),
            jax.ShapeDtypeStruct((edges, inner), F32),
        ),
        in_specs=[SMEM] * 2 + [VMEM] * 5,
        out_specs=(VMEM,) * 6,
        scratch_shapes=[
            pltpu.VMEM((edges, width), F32),
            pltpu.VMEM((edges, width), BF16),
        ],
        compiler_params=PARAMS,
        name="edges_forward",
    )(recv, count, arrived, words, degree, w_in, w_out)


def edges_backward(recv, arrived, mask_t, mask, degree, w_in, w_out, feats, act, gate):
    tiles = arrived.shape[0]
    edges, width, inner = degree.size, w_in.shape[0], w_in.shape[1]
    grad_rows = 2 * inner * width // LANES
    rows = width // LANES * TILE + grad_rows // tiles
    return pl.pallas_call(
        backward_kernel,
        out_shape=jax.ShapeDtypeStruct((tiles, rows, LANES), BF16),
        in_specs=[SMEM] + [VMEM] * 9,
        out_specs=VMEM,
        scratch_shapes=[
            pltpu.VMEM((edges, width), F32),
            pltpu.VMEM((edges, width), BF16),
            pltpu.VMEM((grad_rows, LANES), F32),
        ],
        compiler_params=PARAMS,
        name="edges_backward",
    )(recv, arrived, mask_t, mask, degree, w_in, w_out, feats, act, gate)


def sum_products(send_ref, arrived, acc):
    pieces = acc.shape[1] // LANES
    acc[...] = jnp.zeros_like(acc)

    def body(i, carry):
        for k in range(2 * STEP_TILES):
            source, slot = i * STEP_TILES + k // 2, k % 2
            where = half_at(send_ref[2 * source + slot])
            for h in range(pieces):
                at = (slot * pieces + h) * HALF
                acc[where, h * LANES : (h + 1) * LANES] += arrived[source, at : at + HALF].astype(F32)
        return carry

    lax.fori_loop(0, steps_of(arrived), body, 0)


def grad_kernel(send_ref, arrived, cot_ref, out_ref, acc):
    sum_products(send_ref, arrived, acc)
    out_ref[...] = cot_ref[...].astype(F32) + acc[...]


def node_grads(send, arrived, cot):
    return pl.pallas_call(
        grad_kernel,
        out_shape=jax.ShapeDtypeStruct(cot.shape, F32),
        in_specs=[SMEM, VMEM, VMEM],
        out_specs=VMEM,
        scratch_shapes=[pltpu.VMEM(cot.shape, F32)],
        compiler_params=PARAMS,
        name="node_grads",
    )(send, arrived, cot)


def tail_sum_kernel(arrived_ref, out_ref):
    rows = out_ref.shape[0]
    out_ref[...] = jnp.sum(arrived_ref[:, arrived_ref.shape[1] - rows :].astype(F32), axis=0)


def tail_sum(arrived, rows):
    return pl.pallas_call(
        tail_sum_kernel,
        out_shape=jax.ShapeDtypeStruct((arrived.shape[1] - rows, arrived.shape[2]), F32),
        in_specs=[VMEM],
        out_specs=VMEM,
        compiler_params=PARAMS,
        name="weight_sums",
    )(arrived)


def finish_kernel(
    factors, core_ref, mine, theirs, grads_mine, grads_theirs, updated_mine, updated_theirs,
    updated_ref, nodes_ref, in_ref, out_ref, gain_ref,
):
    edge_factor, node_factor = factors
    owners = mine.shape[0]
    pieces, inner = out_ref.shape[1] // LANES, out_ref.shape[0]
    extra = pieces * inner // owners

    def place(both, grads, updated):
        for c in range(2):
            for block in range(grads_mine.shape[0] // HALF):
                at = (2 * block + c) * HALF
                nodes_ref[at : at + HALF] = grads[c][block * HALF : (block + 1) * HALF]
                updated_ref[at : at + HALF] = updated[c][block * HALF : (block + 1) * HALF]
        for d in range(2 * owners):
            rows = both[d % 2][d // 2, :extra].astype(F32) * edge_factor
            at = d * extra
            if at < pieces * inner:
                lane = at // inner * LANES
                out_ref[at % inner : at % inner + extra, lane : lane + LANES] = rows
            else:
                at -= pieces * inner
                deep = in_ref.shape[0]
                lane = at // deep * LANES
                in_ref[at % deep : at % deep + extra, lane : lane + LANES] = rows
        gains = sum(jnp.sum(half[:, extra:].astype(F32), axis=0) for half in both)
        gain = jnp.concatenate([gains[i : i + 1] + gains[pieces + i : pieces + i + 1] for i in range(pieces)], axis=1)
        gain_ref[...] = gain * node_factor

    @pl.when(core_ref[0] == 0)
    def _():
        place((mine, theirs), (grads_mine, grads_theirs), (updated_mine, updated_theirs))

    @pl.when(core_ref[0] != 0)
    def _():
        place((theirs, mine), (grads_theirs, grads_mine), (updated_theirs, updated_mine))


def finish(core, mine, theirs, grads, updated, inner, factors):
    nodes, width = 2 * grads[0].shape[0], grads[0].shape[1]
    return pl.pallas_call(
        functools.partial(finish_kernel, factors),
        out_shape=(
            jax.ShapeDtypeStruct((nodes, width), BF16),
            jax.ShapeDtypeStruct((nodes, width), F32),
            jax.ShapeDtypeStruct((width, inner), F32),
            jax.ShapeDtypeStruct((inner, width), F32),
            jax.ShapeDtypeStruct((1, width), F32),
        ),
        in_specs=[SMEM] + [VMEM] * 6,
        out_specs=(VMEM,) * 5,
        compiler_params=PARAMS,
        name="finish",
    )(core, mine, theirs, *grads, *updated)


def norm_kernel(
    send_ref, arrived, feats_ref, cot_ref, gain_ref, updated_ref, part_ref, out_ref, acc, d_summed
):
    sum_products(send_ref, arrived, acc)
    gain = gain_ref[...]

    def body(i, part):
        at = rows_at(i)
        summed = acc[at]
        inv_rms = lax.rsqrt(jnp.mean(summed * summed, axis=-1, keepdims=True) + 1e-05)
        normed = summed * inv_rms
        updated_ref[at] = (feats_ref[at].astype(F32) + normed * gain).astype(BF16)
        upstream = cot_ref[at].astype(F32)
        d_normed = upstream * gain
        inner = jnp.mean(d_normed * normed, axis=-1, keepdims=True)
        d_summed[at] = (inv_rms * (d_normed - normed * inner)).astype(BF16)
        return part + jnp.sum((upstream * normed).reshape(TILE // 8, 8, -1), axis=0)

    parts = lax.fori_loop(0, acc.shape[0] // TILE, body, jnp.zeros((8, acc.shape[1]), F32))
    row = jnp.sum(parts, axis=0, keepdims=True)
    high = row.astype(BF16).astype(F32)
    rows = [part[:, i : i + LANES] for part in (high, row - high) for i in range(0, row.shape[1], LANES)]
    rows.append(jnp.zeros((part_ref.shape[0] - len(rows), LANES), F32))
    part_ref[...] = jnp.concatenate(rows, axis=0).astype(BF16)

    select_kernel(send_ref, d_summed, out_ref)


def norm_and_select(send, arrived, feats, cot, gain):
    nodes, width = feats.shape
    devices = arrived.shape[0]
    return pl.pallas_call(
        norm_kernel,
        out_shape=(
            jax.ShapeDtypeStruct((nodes, width), BF16),
            jax.ShapeDtypeStruct((16, LANES), BF16),
            jax.ShapeDtypeStruct((devices, send.shape[0] // devices * HALF, width), BF16),
        ),
        in_specs=[SMEM] + [VMEM] * 4,
        out_specs=(VMEM,) * 3,
        scratch_shapes=[pltpu.VMEM((nodes, width), F32), pltpu.VMEM((nodes, width), BF16)],
        compiler_params=PARAMS,
        name="norm_and_select",
    )(send, arrived, feats, cot, gain)


def exchange(tiles):
    return lax.all_to_all(tiles, ("wide", "narrow"), split_axis=0, concat_axis=0, tiled=True)


def exchange_wide(chunks):
    return lax.all_to_all(chunks, "wide", split_axis=0, concat_axis=0, tiled=True)


def swap(rows):
    return lax.ppermute(rows, "narrow", [(0, 1), (1, 0)])


def shards(
    node_feats,
    send_block,
    recv_block,
    tile_count,
    mask_bits,
    degree,
    weight_in,
    weight_out,
    norm_gain,
    cotangent,
):
    owners = lax.axis_size("wide")
    nodes, width = node_feats.shape
    inner = weight_in.shape[1]
    core = lax.axis_index("narrow")
    devices = 2 * owners
    by_core = lambda mine, theirs: (jnp.where(core == 0, mine, theirs), jnp.where(core == 0, theirs, mine))
    my_slots = send_block[0, :, 0, :]
    send = jnp.stack(by_core(my_slots, swap(my_slots)), 1).reshape(-1)
    recv = recv_block.reshape(-1)
    count = tile_count.reshape(-1)
    words = mask_bits[0, 0].transpose(0, 2, 1, 3)
    degree_rows = degree.reshape(-1, LANES)
    half_of = lambda rows: lax.dynamic_index_in_dim(
        rows.reshape(-1, 2, HALF, width), core, 1, keepdims=False
    ).reshape(-1, width)

    feats_half, cot_half = half_of(node_feats), half_of(cotangent)
    picked, recv, count, words, cot_half = lax.optimization_barrier(
        (select(send, feats_half, devices), recv, count, words, cot_half)
    )
    arrived = exchange(picked)
    products, mask_t, mask, feats, act, gate = edges_forward(
        recv, count, arrived, words, degree_rows, weight_in, weight_out
    )
    updated, gain_part, picked = norm_and_select(send, exchange(products), feats_half, cot_half, norm_gain[None, :])
    arrived = exchange(picked)
    products = edges_backward(recv, arrived, mask_t, mask, degree_rows, weight_in, weight_out, feats, act, gate)
    arrived = exchange(products)

    arrived, updated, gain_part = lax.optimization_barrier((arrived, updated, gain_part))
    weight_sums = tail_sum(arrived, 2 * width // LANES * HALF)
    chunk = jnp.concatenate([weight_sums.astype(BF16), gain_part[: max(8, 2 * width // LANES)]], 0)
    grads_half = node_grads(send, arrived, cot_half)
    grads_other, updated_other, chunk = lax.optimization_barrier((swap(grads_half), swap(updated), chunk))
    everyone = exchange_wide(jnp.broadcast_to(chunk[None], (owners,) + chunk.shape))
    edge_factor = (degree.shape[0] * devices) ** (-0.5)
    node_factor = (nodes * owners) ** (-0.5)
    core_at = core.astype(jnp.int32).reshape(1)
    updated, grad_nodes, grad_in, grad_out, grad_gain = finish(
        core_at,
        everyone,
        swap(everyone),
        (grads_half, grads_other),
        (updated, updated_other),
        inner,
        (edge_factor, node_factor),
    )
    return updated, grad_nodes, grad_in, grad_out, grad_gain.reshape(width)


def solution(mesh):
    return jax.shard_map(
        shards,
        mesh=mesh,
        in_specs=(
            P("wide", None),
            P("wide", None, "narrow", None),
            P("wide", "narrow", None, None),
            P("wide", "narrow", None),
            P("wide", "narrow", None, None, None, None),
            P(("wide", "narrow")),
            P(),
            P(),
            P(),
            P("wide", None),
        ),
        out_specs=(P("wide", None), P("wide", None), P(), P(), P()),
        check_vma=False,
    )
```
